128 devices in a mesh: wide: 16 (over z, y), narrow: 8 (over x, core).
Axes of the slice: x: 4, y: 4, z: 4, core: 2. Of those that a mesh axis runs over, the one named last changes fastest.
Arguments:
- xbc: bfloat16 [65536, 5376], P(('wide', 'narrow')), may hold values from -6 to 6
- conv_weight: float32 [4, 5376], replicated, may hold values from -3 to 3
- conv_bias: float32 [5376], replicated, may hold values from -1 to 0
- dt: float32 [80, 65536], P(None, ('wide', 'narrow')), may hold values from 0 to 1, as said below
- decay_log: float32 [80, 65536], P(None, ('wide', 'narrow')), may hold values from -1 to 0, as said below
- skip: float32 [80], replicated, may hold values from 0.5 to 1.5
Outputs:
- mixed: bfloat16 [65536, 5120], P(('wide', 'narrow'))
The draws below stay inside these ranges and needn't reach their ends.
Inputs may be any that keep to these rules, and one draw needn't show every extreme that they name: `dt`: step sizes are positive. `decay_log`: entries are at most zero.
All inputs are finite; a program needn't handle non-finite values.
Results may differ from the reference program's by a relative error of at most 0.0053.
Values may be sent and summed in bfloat16 or wider, within the bound.
No kernel may reach another device: no remote copies, remote signals or barrier semaphores. Data moves between devices by JAX's collectives and lax.ppermute only.
A program may use at most 704 MiB of HBM per device.

```python
import math
import jax
import jax.numpy as jnp
from jax import lax

MIXER_HEADS = 80
HEAD_DIM = 64
N_STATE = 128
CONV = 4
BLOCK = 256
TOK_DEV = 512
INNER = 5120
SEQUENCE_TOKENS = 65536


def head_rates(key, slow_heads):
    order = jax.random.permutation(jax.random.fold_in(key, 101), MIXER_HEADS)
    slow = order < slow_heads
    slow_rate = jnp.exp(jax.random.uniform(jax.random.fold_in(key, 102), (MIXER_HEADS,), jnp.float32, math.log(0.05), math.log(0.5))) / SEQUENCE_TOKENS
    other_rate = jnp.exp(jax.random.uniform(jax.random.fold_in(key, 103), (MIXER_HEADS,), jnp.float32, math.log(1.0 / (4 * TOK_DEV)), math.log(1.0 / 30)))
    return jnp.where(slow, slow_rate, other_rate)


def draw_decay_log(key, part):
    decay_speeds = head_rates(key, MIXER_HEADS // 2)
    key = jax.random.fold_in(key, 7)
    scattered_rows = jnp.exp(jax.random.uniform(jax.random.fold_in(key, 1), (MIXER_HEADS, SEQUENCE_TOKENS), jnp.float32, math.log(0.5), math.log(2.0)))
    region = jnp.exp(jax.random.uniform(jax.random.fold_in(key, 2), (MIXER_HEADS, SEQUENCE_TOKENS // BLOCK), jnp.float32, math.log(0.5), math.log(2.0)))
    complete_region = jnp.repeat(region, BLOCK, axis=1)
    device_slots = jax.random.randint(jax.random.fold_in(key, 3), (3,), 0, SEQUENCE_TOKENS)
    objective_value = jax.random.uniform(jax.random.fold_in(key, 4), (MIXER_HEADS, 1), jnp.float32, 0.2, 0.4)
    positions = jnp.arange(SEQUENCE_TOKENS, dtype=jnp.int32)
    impulse_hits = jnp.any(positions[None, :] == device_slots[:, None], axis=0)
    spike_input = jnp.where(impulse_hits[None, :], jnp.log(1.0 - objective_value), 0.0)
    return (-decay_speeds[:, None] * scattered_rows * complete_region + spike_input).astype(jnp.float32)


def draw_dt(key, part):
    decay_speeds = head_rates(key, MIXER_HEADS // 2)
    key = jax.random.fold_in(key, 11)
    doubling_level = jnp.exp(jax.random.uniform(jax.random.fold_in(key, 1), (MIXER_HEADS, SEQUENCE_TOKENS), jnp.float32, math.log(0.25), 0.0))
    doubling_factor = doubling_level ** 16
    head_first_index = jnp.minimum(1.0, jnp.sqrt(66.0 * jnp.maximum(decay_speeds, 2.0 / SEQUENCE_TOKENS)))
    return (doubling_factor * head_first_index[:, None]).astype(jnp.float32)


def levels(own_key, dims, split, low, high):
    def one(position, shards_of):
        draws = jax.random.uniform(jax.random.fold_in(jax.random.fold_in(own_key, 6), position), (shards_of,), jnp.float32, low / len(split), high / len(split))
        return jnp.repeat(jnp.exp(draws), dims[position] // shards_of).reshape((-1,) + (1,) * (len(dims) - position - 1))

    loudness = one(*split[0])
    for cut in split[1:]:
        loudness = loudness * one(*cut)
    return loudness


def noise(own_key, extent, spread, limit, pieces=(), held_as=jnp.bfloat16):
    factor_of = levels(own_key, extent, pieces, -0.22, 0.18) if pieces else 1.0
    array = jax.random.normal(own_key, extent, jnp.float32) * spread * factor_of
    return jnp.minimum(jnp.maximum(array, -limit), limit).astype(held_as)


def setup_inputs(seed: int = 0) -> dict:
    keys = jax.random.split(jax.random.key(seed), 7)
    return {
        "xbc": noise(keys[0], (SEQUENCE_TOKENS, INNER + 2 * N_STATE), 1.0, 6.0, ((0, 128),)),
        "conv_weight": noise(keys[1], (CONV, INNER + 2 * N_STATE), CONV ** -0.5, 3.0, (), jnp.float32),
        "conv_bias": jnp.clip(jax.random.uniform(keys[2], (INNER + 2 * N_STATE,), jnp.float32, -1.0, 0.0), -1.0, 0.0),
        "dt": draw_dt(jax.random.fold_in(keys[6], 71), 0),
        "decay_log": draw_decay_log(jax.random.fold_in(keys[6], 71), 0),
        "skip": jnp.clip(jax.random.uniform(keys[5], (MIXER_HEADS,), jnp.float32, 0.5, 1.5), 0.5, 1.5),
    }


def convolve(kernel_span, conv_weight, conv_bias):
    length = kernel_span.shape[0] - CONV + 1
    running = conv_bias[None, :]
    for offset in range(CONV):
        running = running + kernel_span[offset:offset + length].astype(jnp.float32) * conv_weight[offset][None, :]
    return jax.nn.silu(running).astype(jnp.bfloat16)


def block_local(active_flag, step_sizes, log_decays):
    length = active_flag.shape[0]
    values = active_flag[:, :INNER].reshape(length, MIXER_HEADS, HEAD_DIM).astype(jnp.float32)
    inputs = active_flag[:, INNER:INNER + N_STATE]
    readout = active_flag[:, INNER + N_STATE:]
    cumulative = jnp.cumsum(log_decays, axis=1)
    scores = jnp.dot(readout, inputs.T, preferred_element_type=jnp.float32)
    later = lax.broadcasted_iota(jnp.int32, (length, length), 0)
    earlier = lax.broadcasted_iota(jnp.int32, (length, length), 1)
    causal = later >= earlier
    exponent = jnp.minimum(cumulative[:, :, None] - cumulative[:, None, :], 0.0)
    decay = jnp.where(causal[None], jnp.exp(exponent), 0.0)
    weights = (scores[None] * decay * step_sizes[:, None, :]).astype(jnp.bfloat16)
    diagonal_part = jnp.einsum('hts,shp->thp', weights.astype(jnp.float32), values)
    to_end = jnp.exp(cumulative[:, -1:] - cumulative) * step_sizes
    loaded = (to_end[:, :, None] * inputs.astype(jnp.float32)[None]).astype(jnp.bfloat16)
    local_state = jnp.einsum('hsn,shp->hpn', loaded.astype(jnp.float32), values)
    return values, readout, cumulative, diagonal_part, local_state


def finish(values, readout, cumulative, diagonal_part, state_now, skip):
    carried = jnp.einsum('tn,hpn->thp', readout.astype(jnp.float32), state_now, precision=lax.Precision.HIGHEST)
    decay_in = jnp.exp(cumulative).T[:, :, None]
    running = diagonal_part + decay_in * carried + skip[None, :, None] * values
    return running.reshape(values.shape[0], INNER).astype(jnp.bfloat16)


def reference(xbc, conv_weight, conv_bias, dt, decay_log, skip):
    blocks_all = SEQUENCE_TOKENS // BLOCK
    blocks = xbc.reshape(blocks_all, BLOCK, xbc.shape[1])
    step_all = dt.reshape(MIXER_HEADS, blocks_all, BLOCK).transpose(1, 0, 2)
    log_all = decay_log.reshape(MIXER_HEADS, blocks_all, BLOCK).transpose(1, 0, 2)

    def advance(carry_pair, element):
        state_now, previous_rows = carry_pair
        block_rows, step_sizes, log_decays = element
        kernel_span = jnp.concatenate([previous_rows, block_rows], axis=0)
        active_flag = convolve(kernel_span, conv_weight, conv_bias)
        values, readout, cumulative, diagonal_part, local_state = block_local(active_flag, step_sizes, log_decays)
        mixed_block = finish(values, readout, cumulative, diagonal_part, state_now, skip)
        new_state = jnp.exp(cumulative[:, -1])[:, None, None] * state_now + local_state
        return (new_state, block_rows[BLOCK - CONV + 1:]), mixed_block

    initial = (jnp.zeros((MIXER_HEADS, HEAD_DIM, N_STATE), jnp.float32), jnp.zeros((CONV - 1, xbc.shape[1]), jnp.bfloat16))
    _, outputs = lax.scan(advance, initial, (blocks, step_all, log_all))
    return outputs.reshape(SEQUENCE_TOKENS, INNER)
```

```python
import jax
import jax.numpy as jnp
from jax import lax
from jax.experimental import pallas as pl
from jax.experimental.pallas import tpu as pltpu
from jax.sharding import PartitionSpec as P

HEADS = 80
HEAD_DIM = 64
N_STATE = 128
CONV = 4
INNER = 5120
TOK = 512
CHUNK = 128
CHUNKS = TOK // CHUNK
TILE = 512
TILES = INNER // TILE
GROUPS = TILE // 128
ROWS = INNER // 128
SENT = 48
LANES = 128
ALL = ("wide", "narrow")
F32 = jnp.float32
BF16 = jnp.bfloat16


def dot(a, b):
    return jnp.dot(a, b, preferred_element_type=F32)


def dot_nt(a, b, precision=None):
    return lax.dot_general(
        a, b, (((1,), (1,)), ((), ())), preferred_element_type=F32, precision=precision
    )


def iota(shape, dim):
    return lax.broadcasted_iota(jnp.int32, shape, dim)


def split_pair(value):
    high = value.astype(BF16)
    low = (value - high.astype(F32)).astype(BF16)
    return jnp.concatenate([high, low], axis=1)


def pad_heads(value):
    return jnp.concatenate(
        [value, jnp.zeros((value.shape[0], LANES - HEADS), value.dtype)], axis=1
    )


def spread(tile):
    head = iota((2 * LANES, TILE), 0) % LANES
    lane = iota((2 * LANES, TILE), 1) // HEAD_DIM
    return (head == lane + tile * (TILE // HEAD_DIM)).astype(F32).astype(BF16)


def conv_tile(x_ref, rim_ref, weight_ref, bias_ref, span_ref, width):
    span_ref[0:8, 0:width] = rim_ref[...].astype(F32)
    span_ref[8 : 8 + TOK, 0:width] = x_ref[...].astype(F32)
    running = bias_ref[...]
    for k in range(CONV):
        running = running + span_ref[5 + k : 5 + k + TOK, 0:width] * weight_ref[k : k + 1, :]
    half = 0.5 * running
    return (half + half * jnp.tanh(half)).astype(BF16)


def chunk_decays(dt_ref, log_ref, chunk):
    rows, cols = iota((CHUNK, CHUNK), 0), iota((CHUNK, CHUNK), 1)
    lower = (rows >= cols).astype(F32)
    unit = (rows == cols).astype(F32)
    span = slice(chunk * CHUNK, (chunk + 1) * CHUNK)
    cumulative = dot_nt(lower, log_ref[:, span], lax.Precision.HIGHEST)
    steps = dot_nt(unit, dt_ref[:, span], lax.Precision.HIGHEST)
    whole = cumulative[CHUNK - 1 :, :]
    middle = 0.5 * whole
    to_middle = jnp.exp(middle - cumulative) * steps
    from_middle = jnp.exp(cumulative - middle)
    return to_middle, from_middle, whole


def state_kernel(
    x_ref, side_ref, rim_ref, rim_side_ref, weight_ref, weight_side_ref, bias_ref, bias_side_ref,
    dt_ref, log_ref,
    values_ref, side_out_ref, sent_ref, factors_ref, halves_ref,
    span_ref, inputs_ref, held_ref,
):
    tile = pl.program_id(0)

    @pl.when(tile == 0)
    def _():
        side = conv_tile(
            side_ref, rim_side_ref, weight_side_ref, bias_side_ref, span_ref, 2 * N_STATE
        )
        side_out_ref[...] = side
        inputs_ref[...] = side[:, 0:N_STATE].astype(F32).T.astype(BF16)
        totals = []
        for q in range(CHUNKS):
            to_middle, from_middle, whole = chunk_decays(dt_ref, log_ref, q)
            span = slice(q * CHUNK, (q + 1) * CHUNK)
            factors_ref[span, 0 : 2 * LANES] = split_pair(pad_heads(to_middle))
            factors_ref[span, 2 * LANES :] = split_pair(pad_heads(from_middle))
            totals.append(whole)
        all_four = jnp.concatenate(totals + [jnp.zeros((8 - CHUNKS, HEADS), F32)], axis=0)
        halves_ref[...] = split_pair(pad_heads(jnp.exp(0.5 * all_four)))
        decay = pad_heads(jnp.exp(totals[0] + totals[1] + totals[2] + totals[3]))
        high = decay.astype(BF16).astype(F32)
        middle = (decay - high).astype(BF16).astype(F32)
        low = decay - high - middle
        tail = jnp.concatenate([high, middle, low, jnp.zeros((5, LANES), F32)], axis=0)
        sent_ref[:, ROWS:, :] = jnp.broadcast_to(tail[None], (N_STATE, 8, LANES)).astype(BF16)

    values = conv_tile(x_ref, rim_ref, weight_ref, bias_ref, span_ref, TILE)
    values_ref[...] = values
    wide = spread(tile)
    halves = dot(halves_ref[...], wide)
    state = jnp.zeros((N_STATE, TILE), F32)
    for q in range(CHUNKS):
        span = slice(q * CHUNK, (q + 1) * CHUNK)
        scale = dot(factors_ref[span, 0 : 2 * LANES], wide)
        scaled = (values[span].astype(F32) * scale).astype(BF16)
        local = dot(inputs_ref[:, span], scaled)
        half = halves[q : q + 1, :]
        state = half * (half * state + local)
    for g in range(GROUPS):
        held_ref[pl.ds(tile * GROUPS + g, N_STATE, stride=ROWS), :] = state[
            :, g * LANES : (g + 1) * LANES
        ]

    @pl.when(tile == TILES - 1)
    def _():
        def move(n, _):
            sent_ref[n, 0:ROWS, :] = held_ref[
                pl.ds(pl.multiple_of(n * ROWS, 8), ROWS), :
            ].astype(BF16)
            return 0

        lax.fori_loop(0, N_STATE, move, 0)


def scan_kernel(count, pieces_ref, out_ref, decay_ref):
    tails = pieces_ref[:, ROWS:, :].astype(F32)
    decay = jnp.sum(tails, axis=1)
    factors = split_pair(decay)
    for t in range(TILES):
        wide = dot(factors, spread(t))
        for g in range(GROUPS):
            decay_ref[pl.ds(t * GROUPS + g, count, stride=ROWS), :] = wide[
                :, g * LANES : (g + 1) * LANES
            ]

    def step(i, running):
        out_ref[i] = running.astype(BF16)
        piece = pieces_ref[i, 0:ROWS, :].astype(F32)
        return decay_ref[pl.ds(pl.multiple_of(i * ROWS, 8), ROWS), :] * running + piece

    lax.fori_loop(0, count, step, jnp.zeros((ROWS, LANES), F32))


def mix_kernel(
    values_ref, side_ref, factors_ref, halves_ref, start_ref, skip_ref,
    out_ref, both_ref, inputs_ref, held_ref,
):
    tile = pl.program_id(0)

    @pl.when(tile == 0)
    def _():
        side = side_ref[...]
        inputs_ref[...] = side[:, 0:N_STATE].astype(F32).T.astype(BF16)
        rows, cols = iota((CHUNK, CHUNK), 0), iota((CHUNK, CHUNK), 1)
        for q in range(CHUNKS):
            span = slice(q * CHUNK, (q + 1) * CHUNK)
            readout = side[span, N_STATE:]
            scores = dot_nt(readout, side[span, 0:N_STATE])
            both_ref[span, 0:CHUNK] = jnp.where(rows >= cols, scores, 0.0).astype(BF16)
            both_ref[span, CHUNK:] = readout

        def move(n, _):
            held_ref[pl.ds(pl.multiple_of(n * ROWS, 8), ROWS), :] = start_ref[n].astype(F32)
            return 0

        lax.fori_loop(0, N_STATE, move, 0)

    wide = spread(tile)
    halves = dot(halves_ref[...], wide)
    state = jnp.concatenate(
        [
            held_ref[pl.ds(tile * GROUPS + g, N_STATE, stride=ROWS), :]
            for g in range(GROUPS)
        ],
        axis=1,
    )
    for q in range(CHUNKS):
        span = slice(q * CHUNK, (q + 1) * CHUNK)
        values = values_ref[span, :].astype(F32)
        scaled = (values * dot(factors_ref[span, 0 : 2 * LANES], wide)).astype(BF16)
        half = halves[q : q + 1, :]
        begin = half * state
        mixed = dot(both_ref[span, :], jnp.concatenate([scaled, begin.astype(BF16)], axis=0))
        rise = dot(factors_ref[span, 2 * LANES :], wide)
        out_ref[span, :] = (mixed * rise + skip_ref[...] * values).astype(BF16)
        if q < CHUNKS - 1:
            state = half * (begin + dot(inputs_ref[:, span], scaled))


def whole(shape):
    return pl.BlockSpec(shape, lambda j: (0,) * len(shape))


def body(xbc, conv_weight, conv_bias, dt, decay_log, skip):
    count = lax.axis_size(ALL)
    rim = lax.ppermute(xbc[TOK - 8 :], ALL, [(i, i + 1) for i in range(count - 1)])
    bias = conv_bias[None, :]
    column = lambda rows: pl.BlockSpec((rows, TILE), lambda j: (0, j))
    side = lambda rows: pl.BlockSpec((rows, 2 * N_STATE), lambda j: (0, INNER // (2 * N_STATE)))
    big = pltpu.CompilerParams(
        dimension_semantics=("arbitrary",), vmem_limit_bytes=48 * 1024 * 1024
    )
    values, sides, sent, factors, halves = pl.pallas_call(
        state_kernel,
        grid=(TILES,),
        in_specs=[
            column(TOK), side(TOK), column(8), side(8), column(CONV), side(CONV), column(1), side(1),
            whole((HEADS, TOK)), whole((HEADS, TOK)),
        ],
        out_specs=[
            column(TOK), whole((TOK, 2 * N_STATE)), whole((N_STATE, SENT, LANES)),
            whole((TOK, 4 * LANES)), whole((8, 2 * LANES)),
        ],
        out_shape=[
            jax.ShapeDtypeStruct((TOK, INNER), BF16),
            jax.ShapeDtypeStruct((TOK, 2 * N_STATE), BF16),
            jax.ShapeDtypeStruct((N_STATE, SENT, LANES), BF16),
            jax.ShapeDtypeStruct((TOK, 4 * LANES), BF16),
            jax.ShapeDtypeStruct((8, 2 * LANES), BF16),
        ],
        scratch_shapes=[
            pltpu.VMEM((8 + TOK, TILE), F32),
            pltpu.VMEM((N_STATE, TOK), BF16),
            pltpu.VMEM((N_STATE * ROWS, LANES), F32),
        ],
        compiler_params=big,
        name="local_states",
    )(xbc, xbc, rim, rim, conv_weight, conv_weight, bias, bias, dt, decay_log)
    pieces = lax.all_to_all(sent, ALL, 0, 0, tiled=True)
    prefixes = pl.pallas_call(
        lambda *refs: scan_kernel(count, *refs),
        out_shape=jax.ShapeDtypeStruct((count, ROWS, LANES), BF16),
        scratch_shapes=[pltpu.VMEM((count * ROWS, LANES), F32)],
        compiler_params=pltpu.CompilerParams(vmem_limit_bytes=48 * 1024 * 1024),
        name="scan_devices",
    )(pieces)
    starts = lax.all_to_all(prefixes, ALL, 0, 0, tiled=True)
    skips = jnp.repeat(skip, HEAD_DIM)[None, :]
    return pl.pallas_call(
        mix_kernel,
        grid=(TILES,),
        in_specs=[
            column(TOK), whole((TOK, 2 * N_STATE)), whole((TOK, 4 * LANES)),
            whole((8, 2 * LANES)), whole((N_STATE, ROWS, LANES)), column(1),
        ],
        out_specs=column(TOK),
        out_shape=jax.ShapeDtypeStruct((TOK, INNER), BF16),
        scratch_shapes=[
            pltpu.VMEM((TOK, 2 * LANES), BF16),
            pltpu.VMEM((N_STATE, TOK), BF16),
            pltpu.VMEM((N_STATE * ROWS, LANES), F32),
        ],
        compiler_params=big,
        name="mix",
    )(values, sides, factors, halves, starts, skips)


def solution(mesh):
    placed = (P(ALL, None), P(), P(), P(None, ALL), P(None, ALL), P())
    return jax.shard_map(
        body, mesh=mesh, in_specs=placed, out_specs=P(ALL, None), check_vma=False
    )
```

```python
import jax
import jax.numpy as jnp
from jax import lax
from jax.experimental import pallas as pl
from jax.experimental.pallas import tpu as pltpu
from jax.sharding import PartitionSpec as P

HEADS = 80
HEAD_DIM = 64
N_STATE = 128
CONV = 4
INNER = 5120
WIDTH = INNER + 2 * N_STATE
TOK = 512
CHUNK = 128
CHUNKS = TOK // CHUNK
LANES = 128
TILE = 512
TILES = INNER // TILE
GROUPS = TILE // LANES
PIECE = 64
HALF_TILES = TILES // 2
HALF_GROUPS = INNER // LANES // 2
PAIRS = N_STATE // 2
ROWS = 2 * HALF_GROUPS
SENT = ROWS + 8
ALL = ("wide", "narrow")
F32 = jnp.float32
BF16 = jnp.bfloat16
MIB = 1024 * 1024


def dot(a, b):
    return jnp.dot(a, b, preferred_element_type=F32)


def dot_nt(a, b, precision=None):
    return lax.dot_general(
        a, b, (((1,), (1,)), ((), ())), preferred_element_type=F32, precision=precision
    )


def iota(shape, dim):
    return lax.broadcasted_iota(jnp.int32, shape, dim)


def split_pair(value):
    high = value.astype(BF16)
    low = (value - high.astype(F32)).astype(BF16)
    return jnp.concatenate([high, low], axis=1)


def pad_heads(value):
    return jnp.concatenate(
        [value, jnp.zeros((value.shape[0], LANES - HEADS), value.dtype)], axis=1
    )


def spread(tile):
    head = iota((2 * LANES, TILE), 0) % LANES
    lane = iota((2 * LANES, TILE), 1) // HEAD_DIM
    return (head == lane + tile * (TILE // HEAD_DIM)).astype(F32).astype(BF16)


def core_index():
    return lax.rem(lax.axis_index("narrow"), 2)


def running_decay(log_ref, dt_ref, chunk):
    rows, cols = iota((CHUNK, CHUNK), 0), iota((CHUNK, CHUNK), 1)
    lower = (rows >= cols).astype(F32)
    unit = (rows == cols).astype(F32)
    span = slice(chunk * CHUNK, (chunk + 1) * CHUNK)
    cumulative = dot_nt(lower, log_ref[:, span], lax.Precision.HIGHEST)
    steps = dot_nt(unit, dt_ref[:, span], lax.Precision.HIGHEST)
    return cumulative, steps


def thirds(row):
    high = row.astype(BF16).astype(F32)
    middle = (row - high).astype(BF16).astype(F32)
    low = row - high - middle
    return jnp.concatenate([high, middle, low, jnp.zeros((5, LANES), F32)], axis=0)


def fetch_kernel(x_hbm, dt_ref, log_ref, x_ref, to_end_ref, tail_ref, sem):
    copy = pltpu.make_async_copy(x_hbm, x_ref, sem)
    copy.start()
    after = jnp.zeros((1, HEADS), F32)
    for q in reversed(range(CHUNKS)):
        cumulative, steps = running_decay(log_ref, dt_ref, q)
        total = cumulative[CHUNK - 1 :, :]
        to_end = jnp.exp(total - cumulative + after) * steps
        to_end_ref[q * CHUNK : (q + 1) * CHUNK, :] = split_pair(pad_heads(to_end))
        after = after + total
    tail_ref[...] = thirds(pad_heads(jnp.exp(after)))
    copy.wait()


def conv_lanes(x_ref, rim_ref, weight_ref, bias_ref, span_ref, lane, after):
    lanes = pl.ds(lane, LANES)
    span_ref[0:8, :] = rim_ref[:, lanes].astype(F32)
    for row in range(0, TOK, PIECE):
        span_ref[8 + row : 8 + row + PIECE, :] = x_ref[row : row + PIECE, lanes].astype(F32)
    taps = [0.5 * weight_ref[k : k + 1, lanes] for k in range(CONV)]
    start = 0.5 * bias_ref[:, lanes]
    for row in range(0, TOK, PIECE):
        half = start
        for k in range(CONV):
            half = half + span_ref[5 + k + row : 5 + k + row + PIECE, :] * taps[k]
        after((half + half * jnp.tanh(half)).astype(BF16), row)


def tile_lanes(t):
    return pl.ds(pl.multiple_of(t * TILE, TILE), TILE)


def half_of(own):
    return core_index() if own else 1 - core_index()


def side_values(x_ref, rim_ref, weight_ref, bias_ref, span_ref, side_ref, inputs_ref):
    for g in range(2):

        def keep(values, row, g=g):
            side_ref[row : row + PIECE, g * LANES : (g + 1) * LANES] = values

        conv_lanes(
            x_ref, rim_ref, weight_ref, bias_ref, span_ref.at[g], INNER + g * LANES, keep
        )
    inputs_ref[...] = side_ref[:, 0:N_STATE].astype(F32).T.astype(BF16)


def state_kernel(
    own, x_ref, rim_ref, weight_ref, bias_ref, to_end_ref, tail_ref, inputs_ref,
    values_hbm, state_ref, *rest,
):
    span_ref, held_ref, scale_ref, loaded_ref, values_ref, sems = rest[-6:]
    spare_hbm = rest[0]
    half = half_of(own)

    def values_copy(t):
        return pltpu.make_async_copy(
            values_ref.at[t], values_hbm.at[:, tile_lanes(t)], sems.at[t]
        )

    def load(t, slot):
        scale_ref[slot] = dot(to_end_ref[...], spread(half * HALF_TILES + t))
        for g in range(GROUPS):
            lane = pl.multiple_of(half * (INNER // 2) + t * TILE + g * LANES, LANES)
            local = slice(g * LANES, (g + 1) * LANES)

            def keep(values, row, local=local):
                piece = slice(row, row + PIECE)
                values_ref[t, piece, local] = values
                loaded_ref[slot, piece, local] = (
                    values.astype(F32) * scale_ref[slot, piece, local]
                ).astype(BF16)

            conv_lanes(
                x_ref, rim_ref, weight_ref, bias_ref, span_ref.at[slot * GROUPS + g], lane, keep
            )
        values_copy(t).start()

    def finish(t, slot):
        state = dot(inputs_ref[...], loaded_ref[slot])
        for g in range(GROUPS):
            first = t * GROUPS + g
            part = state[:, g * LANES : (g + 1) * LANES]
            held_ref[pl.ds(first, PAIRS, stride=ROWS), :] = part[0:PAIRS]
            held_ref[pl.ds(first + HALF_GROUPS, PAIRS, stride=ROWS), :] = part[PAIRS:]

    load(0, 0)

    def step(pair, _):
        load(2 * pair + 1, 1)
        finish(2 * pair, 0)
        load(2 * pair + 2, 0)
        finish(2 * pair + 1, 1)
        return 0

    lax.fori_loop(0, HALF_TILES // 2, step, 0)
    finish(HALF_TILES - 1, 0)
    state_ref[:, ROWS:, :] = jnp.broadcast_to(tail_ref[...][None], (PAIRS, 8, LANES)).astype(BF16)

    def move(n, _):
        first = pl.multiple_of(n * ROWS, 8)
        state_ref[n, 0:ROWS, :] = held_ref[pl.ds(first, ROWS), :].astype(BF16)
        return 0

    lax.fori_loop(0, PAIRS, move, 0, unroll=8)
    if own:
        state_copy = pltpu.make_async_copy(state_ref, spare_hbm, sems.at[HALF_TILES])
        state_copy.start()
    for t in range(HALF_TILES):
        values_copy(t).wait()
    if own:
        state_copy.wait()


def far_state_kernel(
    x_ref, rim_ref, weight_ref, bias_ref, to_end_ref, tail_ref,
    values_hbm, state_ref, side_ref, inputs_ref, span_ref, *scratch,
):
    side_values(x_ref, rim_ref, weight_ref, bias_ref, span_ref, side_ref, inputs_ref)
    state_kernel(
        False, x_ref, rim_ref, weight_ref, bias_ref, to_end_ref, tail_ref, inputs_ref,
        values_hbm, state_ref, span_ref, *scratch,
    )


def rows_of_heads(count, core):
    row = lax.rem(iota((count, ROWS, LANES), 1), HALF_GROUPS)
    head = iota((count, ROWS, LANES), 2)
    return (head // 2 == row + core * HALF_GROUPS).astype(F32)


def lanes_of_heads():
    head = iota((2 * LANES, LANES), 0)
    return (lax.rem(head, 2) == iota((2 * LANES, LANES), 1) // HEAD_DIM).astype(F32).astype(BF16)


def decay_rows(high, middle, count, core):
    mask = rows_of_heads(count, core)
    both = jnp.concatenate([mask * high, mask * middle], axis=2).astype(BF16)
    return dot(both.reshape(count * ROWS, 2 * LANES), lanes_of_heads())


def join_kernel(mine_ref, got_ref, out_ref, got_hbm, sem):
    core = core_index()
    copy = pltpu.make_async_copy(got_ref, got_hbm, sem)
    copy.start()

    def join(first_ref, second_ref):
        first = first_ref[0, ROWS:, :].astype(F32)
        second = second_ref[0, ROWS:, :].astype(F32)
        decay = decay_rows(second[None, 0:1, :], second[None, 1:2, :], 1, core)
        whole = (first[0:1] + first[1:2] + first[2:3]) * (second[0:1] + second[1:2] + second[2:3])
        out_ref[:, ROWS:, :] = jnp.broadcast_to(thirds(whole)[None], (PAIRS, 8, LANES)).astype(BF16)

        def step(n, _):
            out_ref[n, 0:ROWS, :] = (
                decay * first_ref[n, 0:ROWS, :].astype(F32) + second_ref[n, 0:ROWS, :].astype(F32)
            ).astype(BF16)
            return 0

        lax.fori_loop(0, PAIRS, step, 0, unroll=4)

    pl.when(core == 0)(lambda: join(mine_ref, got_ref))
    pl.when(core == 1)(lambda: join(got_ref, mine_ref))
    copy.wait()


def scan_kernel(count, pieces_ref, out_ref, decay_ref):
    tails = pieces_ref[:, ROWS:, :].astype(F32)
    decay_ref[...] = decay_rows(tails[:, 0:1, :], tails[:, 1:2, :], count, core_index())

    def step(i, running):
        out_ref[i] = running.astype(BF16)
        piece = pieces_ref[i, 0:ROWS, :].astype(F32)
        return decay_ref[pl.ds(pl.multiple_of(i * ROWS, 8), ROWS), :] * running + piece

    lax.fori_loop(0, count, step, jnp.zeros((ROWS, LANES), F32), unroll=4)


def unpack(state_ref, held_ref):
    def move(n, _):
        first = pl.multiple_of(n * ROWS, 8)
        held_ref[pl.ds(first, ROWS), :] = state_ref[n, 0:ROWS, :].astype(F32)
        return 0

    lax.fori_loop(0, PAIRS, move, 0, unroll=8)


def state_tile(held_ref, t):
    parts = []
    for g in range(GROUPS):
        first = t * GROUPS + g
        parts.append(
            jnp.concatenate(
                [
                    held_ref[pl.ds(first, PAIRS, stride=ROWS), :],
                    held_ref[pl.ds(first + HALF_GROUPS, PAIRS, stride=ROWS), :],
                ],
                axis=0,
            )
        )
    return jnp.concatenate(parts, axis=1)


def factor_values(
    side_ref, dt_ref, log_ref, first_decay, skip_ref,
    both_ref, inputs_ref, factors_ref, halves_ref, rise_ref,
):
    side = side_ref[...]
    inputs_ref[...] = side[:, 0:N_STATE].astype(F32).T.astype(BF16)
    rows, cols = iota((CHUNK, CHUNK), 0), iota((CHUNK, CHUNK), 1)
    before = jnp.zeros((1, HEADS), F32)
    for q in range(CHUNKS):
        span = slice(q * CHUNK, (q + 1) * CHUNK)
        readout = side[span, N_STATE:]
        scores = dot_nt(readout, side[span, 0:N_STATE])
        both_ref[span, 0:CHUNK] = jnp.where(rows >= cols, scores, 0.0).astype(BF16)
        both_ref[span, CHUNK:] = readout
        cumulative, steps = running_decay(log_ref, dt_ref, q)
        total = cumulative[CHUNK - 1 :, :]
        middle = 0.5 * total
        factors_ref[span, 0 : 2 * LANES] = split_pair(
            pad_heads(jnp.exp(middle - cumulative) * steps)
        )
        factors_ref[span, 2 * LANES :] = split_pair(pad_heads(jnp.exp(cumulative - middle)))
        rise_ref[span, :] = split_pair(pad_heads(jnp.exp(cumulative + before) * first_decay))
        before = before + total
        halves_ref[8 * q : 8 * q + 8, :] = split_pair(
            jnp.broadcast_to(pad_heads(jnp.exp(middle)), (8, LANES))
        )
    halves_ref[8 * CHUNKS :, :] = split_pair(jnp.broadcast_to(pad_heads(skip_ref[...]), (8, LANES)))


def far_local_kernel(*refs):
    local_kernel(False, None, *refs)


def own_local_kernel(
    values_hbm, side_ref, dt_ref, log_ref, skip_ref, start_hbm,
    part_hbm, both_ref, inputs_ref, factors_ref, halves_ref, rise_ref,
    *scratch,
):
    def prepare(start_ref):
        tail = start_ref[0, ROWS:, 0:HEADS].astype(F32)
        first_decay = jnp.where(core_index() == 0, 1.0, tail[0:1] + tail[1:2] + tail[2:3])
        factor_values(
            side_ref, dt_ref, log_ref, first_decay, skip_ref,
            both_ref, inputs_ref, factors_ref, halves_ref, rise_ref,
        )

    local_kernel(
        True, prepare, values_hbm, both_ref, inputs_ref, factors_ref, halves_ref, start_hbm,
        part_hbm, *scratch,
    )


def local_kernel(
    own, prepare, values_hbm, both_ref, inputs_ref, factors_ref, halves_ref, start_hbm,
    part_hbm,
    held_ref, scaled_ref, start_ref, values_ref, part_ref, scale_ref, rise_ref, in_sems, out_sems,
):
    half = half_of(own)
    start_copy = pltpu.make_async_copy(start_hbm, start_ref, in_sems.at[HALF_TILES])
    start_copy.start()

    def values_copy(t):
        return pltpu.make_async_copy(
            values_hbm.at[:, t * TILE : (t + 1) * TILE], values_ref.at[t], in_sems.at[t]
        )

    def part_copy(t):
        return pltpu.make_async_copy(
            part_ref.at[t], part_hbm.at[:, t * TILE : (t + 1) * TILE], out_sems.at[t]
        )

    for t in range(HALF_TILES):
        values_copy(t).start()
    start_copy.wait()
    if own:
        prepare(start_ref)

    @pl.when(core_index() == 0)
    def _():
        held_ref[...] = jnp.zeros_like(held_ref)

    pl.when(core_index() == 1)(lambda: unpack(start_ref, held_ref))
    for t in range(HALF_TILES):
        wide = spread(half * HALF_TILES + t)
        halves = dot(halves_ref[...], wide)
        skips = halves[8 * CHUNKS : 8 * CHUNKS + 1, :]
        state = state_tile(held_ref, t)
        values_copy(t).wait()
        scale_ref[...] = dot(factors_ref[:, 0 : 2 * LANES], wide)
        rise_ref[...] = dot(factors_ref[:, 2 * LANES :], wide)
        for q in range(CHUNKS):
            span = slice(q * CHUNK, (q + 1) * CHUNK)
            values = values_ref[t, span, :].astype(F32)
            scaled_ref[q] = (values * scale_ref[span, :]).astype(BF16)
            step = halves[8 * q : 8 * q + 1, :]
            begin = step * state
            mixed = dot(
                both_ref[span, :], jnp.concatenate([scaled_ref[q], begin.astype(BF16)], axis=0)
            )
            part_ref[t, span, :] = (
                mixed * rise_ref[span, :] + skips * values
            )
            if q < CHUNKS - 1:
                state = step * (begin + dot(inputs_ref[:, span], scaled_ref[q]))
        part_copy(t).start()
    for t in range(HALF_TILES):
        part_copy(t).wait()


def mix_kernel(
    own, part_hbm, side_ref, rise_ref, start_ref, *rest
):
    out_hbm, held_ref, part_ref, ready_ref, in_sems, out_sems = rest[-6:]
    half = half_of(own)

    def part_copy(t):
        return pltpu.make_async_copy(
            part_hbm.at[:, t * TILE : (t + 1) * TILE], part_ref.at[t], in_sems.at[t]
        )

    def out_copy(t):
        lanes = pl.ds(pl.multiple_of(half * (INNER // 2) + t * TILE, TILE), TILE)
        return pltpu.make_async_copy(ready_ref.at[t], out_hbm.at[:, lanes], out_sems.at[t])

    for t in range(HALF_TILES):
        part_copy(t).start()
    unpack(start_ref, held_ref)
    for t in range(HALF_TILES):
        wide = spread(half * HALF_TILES + t)
        state = state_tile(held_ref, t).astype(BF16)
        part_copy(t).wait()
        for q in range(CHUNKS):
            span = slice(q * CHUNK, (q + 1) * CHUNK)
            carried = dot(side_ref[span, N_STATE:], state)
            ready_ref[t, span, :] = (
                part_ref[t, span, :] + dot(rise_ref[span, :], wide) * carried
            ).astype(BF16)
        out_copy(t).start()
    for t in range(HALF_TILES):
        out_copy(t).wait()


VMEM = pl.BlockSpec(memory_space=pltpu.VMEM)
HBM = pl.BlockSpec(memory_space=pltpu.HBM)


def params(limit):
    return pltpu.CompilerParams(vmem_limit_bytes=limit * MIB)


def in_hbm(value):
    return pltpu.with_memory_space_constraint(value, pltpu.HBM)


def body(xbc, conv_weight, conv_bias, dt, decay_log, skip):
    count = lax.axis_size(ALL)
    chips = count // 2
    swap = [(i, i ^ 1) for i in range(lax.axis_size("narrow"))]
    onward = [(i, i + 1) for i in range(0, lax.axis_size("narrow"), 2)]
    groups = [[2 * c + k for c in range(chips)] for k in range(2)]
    state_out = pltpu.VMEM((PAIRS, SENT, LANES), BF16)
    state_hbm = pltpu.HBM((PAIRS, SENT, LANES), BF16)
    half_out = pltpu.HBM((TOK, INNER // 2), BF16)
    held = pltpu.VMEM((PAIRS * ROWS, LANES), F32)
    tiles_16 = pltpu.VMEM((HALF_TILES, TOK, TILE), BF16)
    tiles_32 = pltpu.VMEM((HALF_TILES, TOK, TILE), F32)
    tile_sems = pltpu.SemaphoreType.DMA((HALF_TILES,))
    inputs_out = jax.ShapeDtypeStruct((N_STATE, TOK), BF16)
    pair_out = jax.ShapeDtypeStruct((TOK, 2 * LANES), BF16)

    rim = lax.ppermute(xbc[TOK - 8 :], ALL, [(i, i + 1) for i in range(count - 1)])
    x_near, to_end, tail = pl.pallas_call(
        fetch_kernel,
        in_specs=[HBM, VMEM, VMEM],
        out_specs=[VMEM] * 3,
        out_shape=[pltpu.VMEM((TOK, WIDTH), BF16), pair_out, pltpu.VMEM((8, LANES), F32)],
        scratch_shapes=[pltpu.SemaphoreType.DMA],
        compiler_params=params(8),
        name="fetch",
    )(in_hbm(xbc), in_hbm(dt), in_hbm(decay_log))
    bias = conv_bias[None, :]
    state_scratch = [
        pltpu.VMEM((2 * GROUPS, 8 + TOK, LANES), F32),
        held,
        pltpu.VMEM((2, TOK, TILE), F32),
        pltpu.VMEM((2, TOK, TILE), BF16),
        tiles_16,
        pltpu.SemaphoreType.DMA((HALF_TILES + 1,)),
    ]
    values_far, other, side, inputs = pl.pallas_call(
        far_state_kernel,
        in_specs=[VMEM] * 6,
        out_specs=[HBM, VMEM, VMEM, VMEM],
        out_shape=[half_out, state_out, pair_out, inputs_out],
        scratch_shapes=state_scratch,
        compiler_params=params(16),
        name="far_states",
    )(x_near, rim, conv_weight, bias, to_end, tail)
    got = lax.ppermute(other, "narrow", swap)
    x_near, other = lax.optimization_barrier((x_near, other))
    values_own, mine, spare = pl.pallas_call(
        lambda *refs: state_kernel(True, *refs),
        in_specs=[VMEM] * 7,
        out_specs=[HBM, VMEM, HBM],
        out_shape=[half_out, state_out, state_hbm],
        scratch_shapes=state_scratch,
        compiler_params=params(16),
        cost_estimate=pl.CostEstimate(flops=2 * 10**9, bytes_accessed=10**7, transcendentals=0),
        name="own_states",
    )(x_near, rim, conv_weight, bias, to_end, tail, inputs)
    got, mine = lax.optimization_barrier((got, mine))
    joined, got = pl.pallas_call(
        join_kernel,
        in_specs=[VMEM] * 2,
        out_specs=[VMEM, HBM],
        out_shape=[jax.ShapeDtypeStruct((PAIRS, SENT, LANES), BF16), state_hbm],
        scratch_shapes=[pltpu.SemaphoreType.DMA],
        compiler_params=params(8),
        name="join_cores",
    )(mine, got)
    pieces = lax.all_to_all(joined, ALL, 0, 0, axis_index_groups=groups, tiled=True)
    joined, side = lax.optimization_barrier((joined, side))
    local_scratch = [
        held,
        pltpu.VMEM((CHUNKS, CHUNK, TILE), BF16),
        pltpu.VMEM((PAIRS, SENT, LANES), BF16),
        tiles_16,
        tiles_32,
        pltpu.VMEM((TOK, TILE), F32),
        pltpu.VMEM((TOK, TILE), F32),
        pltpu.SemaphoreType.DMA((HALF_TILES + 1,)),
        tile_sems,
    ]
    part_out = pltpu.HBM((TOK, INNER // 2), F32)
    part_own, both, inputs, factors, halves, rise = pl.pallas_call(
        own_local_kernel,
        in_specs=[HBM] + [VMEM] * 4 + [HBM],
        out_specs=[HBM] + [VMEM] * 5,
        out_shape=[
            part_out,
            pair_out,
            inputs_out,
            jax.ShapeDtypeStruct((TOK, 4 * LANES), BF16),
            jax.ShapeDtypeStruct((8 * CHUNKS + 8, 2 * LANES), BF16),
            pair_out,
        ],
        scratch_shapes=local_scratch,
        compiler_params=params(22),
        cost_estimate=pl.CostEstimate(flops=10**6, bytes_accessed=10**5, transcendentals=0),
        name="own_part",
    )(in_hbm(values_own), side, in_hbm(dt), in_hbm(decay_log), skip[None, :], in_hbm(got))
    pieces, part_own = lax.optimization_barrier((pieces, part_own))
    prefixes = pl.pallas_call(
        lambda *refs: scan_kernel(chips, *refs),
        in_specs=[VMEM],
        out_specs=VMEM,
        out_shape=jax.ShapeDtypeStruct((chips, ROWS, LANES), BF16),
        scratch_shapes=[pltpu.VMEM((chips * ROWS, LANES), F32)],
        compiler_params=params(12),
        name="scan_chips",
    )(pieces)
    own = lax.all_to_all(prefixes, ALL, 0, 0, axis_index_groups=groups, tiled=True)
    prefixes, values_far = lax.optimization_barrier((prefixes, values_far))
    prefixes, spare = lax.optimization_barrier((prefixes, spare))
    before = lax.ppermute(spare, "narrow", onward)
    part_far = pl.pallas_call(
        far_local_kernel,
        in_specs=[HBM] + [VMEM] * 4 + [HBM],
        out_specs=HBM,
        out_shape=part_out,
        scratch_shapes=local_scratch,
        compiler_params=params(22),
        cost_estimate=pl.CostEstimate(flops=10**6, bytes_accessed=10**5, transcendentals=0),
        name="far_part",
    )(in_hbm(values_far), both, inputs, factors, halves, in_hbm(before))
    own, part_far = lax.optimization_barrier((own, part_far))
    across = lax.ppermute(own, "narrow", swap)

    def mix(own, part, start, *out):
        return pl.pallas_call(
            lambda *refs: mix_kernel(own, *refs),
            in_specs=[HBM] + [VMEM] * 3 + [HBM] * len(out),
            out_specs=HBM,
            out_shape=jax.ShapeDtypeStruct((TOK, INNER), BF16),
            scratch_shapes=[held, tiles_32, tiles_16, tile_sems, tile_sems],
            input_output_aliases={4: 0} if out else {},
            compiler_params=params(16),
            cost_estimate=pl.CostEstimate(
                flops=10**9, bytes_accessed=10**7, transcendentals=0
            ),
            name="own_mix" if own else "far_mix",
        )(in_hbm(part), side, rise, start, *out)

    out = mix(True, part_own, own)
    across, out = lax.optimization_barrier((across, out))
    return mix(False, part_far, across, out)


def solution(mesh):
    placed = (P(ALL, None), P(), P(), P(None, ALL), P(None, ALL), P())
    return jax.shard_map(
        body, mesh=mesh, in_specs=placed, out_specs=P(ALL, None), check_vma=False
    )
```

```python
import jax
import jax.numpy as jnp
from jax import lax
from jax.experimental import pallas as pl
from jax.experimental.pallas import tpu as pltpu
from jax.sharding import PartitionSpec as P

HEADS = 80
HEAD_DIM = 64
N_STATE = 128
CONV = 4
INNER = 5120
WIDTH = INNER + 2 * N_STATE
TOK = 512
CHUNK = 128
CHUNKS = TOK // CHUNK
LANES = 128
TILE = 512
TILES = INNER // TILE
GROUPS = TILE // LANES
PIECE = 64
HALF_TILES = TILES // 2
HEAD_TILES = 2
BATCH = 16
HALF_GROUPS = INNER // LANES // 2
PAIRS = N_STATE // 2
ROWS = 2 * HALF_GROUPS
SENT = ROWS + 8
ALL = ("wide", "narrow")
F32 = jnp.float32
BF16 = jnp.bfloat16
MIB = 1024 * 1024


def dot(a, b):
    return jnp.dot(a, b, preferred_element_type=F32)


def dot_nt(a, b, precision=None):
    return lax.dot_general(
        a, b, (((1,), (1,)), ((), ())), preferred_element_type=F32, precision=precision
    )


def iota(shape, dim):
    return lax.broadcasted_iota(jnp.int32, shape, dim)


def split_pair(value):
    high = value.astype(BF16)
    low = (value - high.astype(F32)).astype(BF16)
    return jnp.concatenate([high, low], axis=1)


def pad_heads(value):
    return jnp.concatenate(
        [value, jnp.zeros((value.shape[0], LANES - HEADS), value.dtype)], axis=1
    )


def spread(tile):
    head = iota((2 * LANES, TILE), 0) % LANES
    lane = iota((2 * LANES, TILE), 1) // HEAD_DIM
    return (head == lane + tile * (TILE // HEAD_DIM)).astype(F32).astype(BF16)


def core_index():
    return lax.rem(lax.axis_index("narrow"), 2)


def running_decay(log_ref, dt_ref, chunk):
    rows, cols = iota((CHUNK, CHUNK), 0), iota((CHUNK, CHUNK), 1)
    lower = (rows >= cols).astype(F32)
    unit = (rows == cols).astype(F32)
    span = slice(chunk * CHUNK, (chunk + 1) * CHUNK)
    cumulative = dot_nt(lower, log_ref[:, span], lax.Precision.HIGHEST)
    steps = dot_nt(unit, dt_ref[:, span], lax.Precision.HIGHEST)
    return cumulative, steps


def thirds(row):
    high = row.astype(BF16).astype(F32)
    middle = (row - high).astype(BF16).astype(F32)
    low = row - high - middle
    return jnp.concatenate([high, middle, low, jnp.zeros((5, LANES), F32)], axis=0)


def fetch_kernel(
    x_hbm, dt_ref, log_ref, skip_ref,
    x_ref, to_end_ref, tail_ref, factors_ref, halves_ref, level_ref, sem,
):
    copy = pltpu.make_async_copy(x_hbm, x_ref, sem)
    copy.start()
    decays = [running_decay(log_ref, dt_ref, q) for q in range(CHUNKS)]
    totals = [cumulative[CHUNK - 1 :, :] for cumulative, _ in decays]
    after = jnp.zeros((1, HEADS), F32)
    for q in reversed(range(CHUNKS)):
        cumulative, steps = decays[q]
        to_end = jnp.exp(totals[q] - cumulative + after) * steps
        to_end_ref[q * CHUNK : (q + 1) * CHUNK, :] = split_pair(pad_heads(to_end))
        after = after + totals[q]
    tail_ref[...] = thirds(pad_heads(jnp.exp(after)))
    before = jnp.zeros((1, HEADS), F32)
    for q in range(CHUNKS):
        span = slice(q * CHUNK, (q + 1) * CHUNK)
        cumulative, steps = decays[q]
        middle = 0.5 * totals[q]
        factors_ref[span, 0 : 2 * LANES] = split_pair(
            pad_heads(jnp.exp(middle - cumulative) * steps)
        )
        factors_ref[span, 2 * LANES :] = split_pair(pad_heads(jnp.exp(cumulative - middle)))
        level_ref[span, :] = pad_heads(jnp.exp(cumulative + before))
        before = before + totals[q]
        halves_ref[8 * q : 8 * q + 8, :] = split_pair(
            jnp.broadcast_to(pad_heads(jnp.exp(middle)), (8, LANES))
        )
    halves_ref[8 * CHUNKS :, :] = split_pair(jnp.broadcast_to(pad_heads(skip_ref[...]), (8, LANES)))
    copy.wait()


def conv_lanes(x_ref, rim_ref, weight_ref, bias_ref, span_ref, lane, after):
    lanes = pl.ds(lane, LANES)
    span_ref[0:8, :] = rim_ref[:, lanes].astype(F32)
    for row in range(0, TOK, PIECE):
        span_ref[8 + row : 8 + row + PIECE, :] = x_ref[row : row + PIECE, lanes].astype(F32)
    taps = [0.5 * weight_ref[k : k + 1, lanes] for k in range(CONV)]
    start = 0.5 * bias_ref[:, lanes]
    for row in range(0, TOK, PIECE):
        half = start
        for k in range(CONV):
            half = half + span_ref[5 + k + row : 5 + k + row + PIECE, :] * taps[k]
        after((half + half * jnp.tanh(half)).astype(BF16), row)


def half_of(own):
    return core_index() if own else 1 - core_index()


def side_values(x_ref, rim_ref, weight_ref, bias_ref, span_ref, side_ref, inputs_ref):
    for g in range(2):

        def keep(values, row, g=g):
            side_ref[row : row + PIECE, g * LANES : (g + 1) * LANES] = values

        conv_lanes(
            x_ref, rim_ref, weight_ref, bias_ref, span_ref.at[g], INNER + g * LANES, keep
        )
    inputs_ref[...] = side_ref[:, 0:N_STATE].astype(F32).T.astype(BF16)


def state_kernel(
    own, x_ref, rim_ref, weight_ref, bias_ref, to_end_ref, tail_ref, inputs_ref,
    values_hbm, state_ref, *rest,
):
    span_ref, held_ref, scale_ref, loaded_ref, values_ref, sems = rest[-6:]
    spare_hbm = rest[0]
    half = half_of(own)

    def values_copy(t):
        return pltpu.make_async_copy(
            values_ref.at[t], values_hbm.at[t], sems.at[t]
        )

    def load(t, slot):
        scale_ref[slot] = dot(to_end_ref[...], spread(half * HALF_TILES + t))
        for g in range(GROUPS):
            lane = pl.multiple_of(half * (INNER // 2) + t * TILE + g * LANES, LANES)
            local = slice(g * LANES, (g + 1) * LANES)

            def keep(values, row, local=local):
                piece = slice(row, row + PIECE)
                values_ref[t, piece, local] = values
                loaded_ref[slot, piece, local] = (
                    values.astype(F32) * scale_ref[slot, piece, local]
                ).astype(BF16)

            conv_lanes(
                x_ref, rim_ref, weight_ref, bias_ref, span_ref.at[slot * GROUPS + g], lane, keep
            )
        values_copy(t).start()

    def finish(t, slot):
        state = dot(inputs_ref[...], loaded_ref[slot])
        for g in range(GROUPS):
            first = t * GROUPS + g
            part = state[:, g * LANES : (g + 1) * LANES]
            held_ref[pl.ds(first, PAIRS, stride=ROWS), :] = part[0:PAIRS]
            held_ref[pl.ds(first + HALF_GROUPS, PAIRS, stride=ROWS), :] = part[PAIRS:]

    load(0, 0)

    def step(pair, _):
        load(2 * pair + 1, 1)
        finish(2 * pair, 0)
        load(2 * pair + 2, 0)
        finish(2 * pair + 1, 1)
        return 0

    lax.fori_loop(0, HALF_TILES // 2, step, 0)
    finish(HALF_TILES - 1, 0)
    state_ref[:, ROWS:, :] = jnp.broadcast_to(tail_ref[...][None], (PAIRS, 8, LANES)).astype(BF16)

    def move(n, _):
        first = pl.multiple_of(n * ROWS, 8)
        state_ref[n, 0:ROWS, :] = held_ref[pl.ds(first, ROWS), :].astype(BF16)
        return 0

    lax.fori_loop(0, PAIRS, move, 0, unroll=8)
    if own:
        state_copy = pltpu.make_async_copy(state_ref, spare_hbm, sems.at[HALF_TILES])
        state_copy.start()
    for t in range(HALF_TILES):
        values_copy(t).wait()
    if own:
        state_copy.wait()


def far_state_kernel(
    x_ref, rim_ref, weight_ref, bias_ref, to_end_ref, tail_ref,
    values_hbm, state_ref, side_ref, inputs_ref, span_ref, *scratch,
):
    side_values(x_ref, rim_ref, weight_ref, bias_ref, span_ref, side_ref, inputs_ref)
    state_kernel(
        False, x_ref, rim_ref, weight_ref, bias_ref, to_end_ref, tail_ref, inputs_ref,
        values_hbm, state_ref, span_ref, *scratch,
    )


def rows_of_heads(count, core):
    row = lax.rem(iota((count, ROWS, LANES), 1), HALF_GROUPS)
    head = iota((count, ROWS, LANES), 2)
    return (head // 2 == row + core * HALF_GROUPS).astype(F32)


def lanes_of_heads():
    head = iota((2 * LANES, LANES), 0)
    return (lax.rem(head, 2) == iota((2 * LANES, LANES), 1) // HEAD_DIM).astype(F32).astype(BF16)


def decay_rows(high, middle, count, core):
    mask = rows_of_heads(count, core)
    both = jnp.concatenate([mask * high, mask * middle], axis=2).astype(BF16)
    return dot(both.reshape(count * ROWS, 2 * LANES), lanes_of_heads())


def join_kernel(mine_ref, got_ref, out_hbm, got_hbm, out_ref, sems):
    core = core_index()
    copy = pltpu.make_async_copy(got_ref, got_hbm, sems.at[PAIRS // BATCH])
    copy.start()

    def out_copy(batch):
        some = pl.ds(batch * BATCH, BATCH)
        return pltpu.make_async_copy(out_ref.at[some], out_hbm.at[some], sems.at[batch])

    def join(first_ref, second_ref):
        first = first_ref[0, ROWS:, :].astype(F32)
        second = second_ref[0, ROWS:, :].astype(F32)
        decay = decay_rows(second[None, 0:1, :], second[None, 1:2, :], 1, core)
        whole = (first[0:1] + first[1:2] + first[2:3]) * (second[0:1] + second[1:2] + second[2:3])
        out_ref[:, ROWS:, :] = jnp.broadcast_to(thirds(whole)[None], (PAIRS, 8, LANES)).astype(BF16)

        def step(n, _):
            out_ref[n, 0:ROWS, :] = (
                decay * first_ref[n, 0:ROWS, :].astype(F32) + second_ref[n, 0:ROWS, :].astype(F32)
            ).astype(BF16)
            return 0

        def some(batch, _):
            lax.fori_loop(0, BATCH, lambda i, c: step(batch * BATCH + i, c), 0, unroll=4)
            out_copy(batch).start()
            return 0

        lax.fori_loop(0, PAIRS // BATCH, some, 0)

    pl.when(core == 0)(lambda: join(mine_ref, got_ref))
    pl.when(core == 1)(lambda: join(got_ref, mine_ref))
    for batch in range(PAIRS // BATCH):
        out_copy(batch).wait()
    copy.wait()


def scan_kernel(count, pieces_ref, out_hbm, out_ref, decay_ref, sems):
    tails = pieces_ref[:, ROWS:, :].astype(F32)
    decay_ref[...] = decay_rows(tails[:, 0:1, :], tails[:, 1:2, :], count, core_index())

    def out_copy(batch):
        some = pl.ds(batch * BATCH, BATCH)
        return pltpu.make_async_copy(out_ref.at[some], out_hbm.at[some], sems.at[batch])

    def step(i, running):
        out_ref[i] = running.astype(BF16)
        piece = pieces_ref[i, 0:ROWS, :].astype(F32)
        return decay_ref[pl.ds(pl.multiple_of(i * ROWS, 8), ROWS), :] * running + piece

    def some(batch, running):
        running = lax.fori_loop(
            0, BATCH, lambda i, held: step(batch * BATCH + i, held), running, unroll=4
        )
        out_copy(batch).start()
        return running

    lax.fori_loop(0, count // BATCH, some, jnp.zeros((ROWS, LANES), F32))
    for batch in range(count // BATCH):
        out_copy(batch).wait()


def unpack(state_ref, held_ref):
    def move(n, _):
        first = pl.multiple_of(n * ROWS, 8)
        held_ref[pl.ds(first, ROWS), :] = state_ref[n, 0:ROWS, :].astype(F32)
        return 0

    lax.fori_loop(0, PAIRS, move, 0, unroll=8)


def state_tile(held_ref, t):
    parts = []
    for g in range(GROUPS):
        first = t * GROUPS + g
        parts.append(
            jnp.concatenate(
                [
                    held_ref[pl.ds(first, PAIRS, stride=ROWS), :],
                    held_ref[pl.ds(first + HALF_GROUPS, PAIRS, stride=ROWS), :],
                ],
                axis=0,
            )
        )
    return jnp.concatenate(parts, axis=1)


def shared_scores(side_ref, both_ref):
    side = side_ref[...]
    rows, cols = iota((CHUNK, CHUNK), 0), iota((CHUNK, CHUNK), 1)
    for q in range(CHUNKS):
        span = slice(q * CHUNK, (q + 1) * CHUNK)
        readout = side[span, N_STATE:]
        scores = dot_nt(readout, side[span, 0:N_STATE])
        both_ref[span, 0:CHUNK] = jnp.where(rows >= cols, scores, 0.0).astype(BF16)
        both_ref[span, CHUNK:] = readout


def far_local_kernel(
    values_hbm, part_own_hbm, both_ref, inputs_ref, factors_ref, halves_ref, start_hbm,
    part_hbm, head_ref, *scratch,
):
    copy = pltpu.make_async_copy(part_own_hbm.at[0:HEAD_TILES], head_ref, scratch[-1])
    copy.start()
    local_kernel(
        False, None, values_hbm, both_ref, inputs_ref, factors_ref, halves_ref, start_hbm,
        part_hbm, *scratch[:-1],
    )
    copy.wait()


def own_local_kernel(
    values_hbm, side_ref, level_ref, inputs_ref, factors_ref, halves_ref, start_hbm,
    part_hbm, both_ref, rise_ref,
    *scratch,
):
    def prepare(start_ref):
        tail = start_ref[0, ROWS:, :].astype(F32)
        first_decay = jnp.where(core_index() == 0, 1.0, tail[0:1] + tail[1:2] + tail[2:3])
        rise_ref[...] = split_pair(level_ref[...] * first_decay)
        shared_scores(side_ref, both_ref)

    local_kernel(
        True, prepare, values_hbm, both_ref, inputs_ref, factors_ref, halves_ref, start_hbm,
        part_hbm, *scratch,
    )


def local_kernel(
    own, prepare, values_hbm, both_ref, inputs_ref, factors_ref, halves_ref, start_hbm,
    part_hbm,
    held_ref, scaled_ref, start_ref, values_ref, part_ref, scale_ref, rise_ref, in_sems, out_sems,
):
    half = half_of(own)
    start_copy = pltpu.make_async_copy(start_hbm, start_ref, in_sems.at[HALF_TILES])
    start_copy.start()

    def values_copy(t):
        return pltpu.make_async_copy(
            values_hbm.at[t], values_ref.at[t], in_sems.at[t]
        )

    def part_copy(t):
        return pltpu.make_async_copy(
            part_ref.at[t], part_hbm.at[t], out_sems.at[t]
        )

    for t in range(HALF_TILES):
        values_copy(t).start()
    start_copy.wait()
    if own:
        prepare(start_ref)

    @pl.when(core_index() == 0)
    def _():
        held_ref[...] = jnp.zeros_like(held_ref)

    pl.when(core_index() == 1)(lambda: unpack(start_ref, held_ref))
    for t in range(HALF_TILES):
        wide = spread(half * HALF_TILES + t)
        halves = dot(halves_ref[...], wide)
        skips = halves[8 * CHUNKS : 8 * CHUNKS + 1, :]
        state = state_tile(held_ref, t)
        values_copy(t).wait()
        scale_ref[...] = dot(factors_ref[:, 0 : 2 * LANES], wide)
        rise_ref[...] = dot(factors_ref[:, 2 * LANES :], wide)
        for q in range(CHUNKS):
            span = slice(q * CHUNK, (q + 1) * CHUNK)
            values = values_ref[t, span, :].astype(F32)
            scaled_ref[q] = (values * scale_ref[span, :]).astype(BF16)
            step = halves[8 * q : 8 * q + 1, :]
            begin = step * state
            mixed = dot(
                both_ref[span, :], jnp.concatenate([scaled_ref[q], begin.astype(BF16)], axis=0)
            )
            part_ref[t, span, :] = (mixed * rise_ref[span, :] + skips * values).astype(BF16)
            if q < CHUNKS - 1:
                state = step * (begin + dot(inputs_ref[:, span], scaled_ref[q]))
        part_copy(t).start()
    for t in range(HALF_TILES):
        part_copy(t).wait()


def own_mix_kernel(
    head_ref, part_hbm, far_part_hbm, side_ref, rise_ref, start_ref,
    out_hbm, far_part_ref, held_ref, ready_ref, part_ref, in_sems, out_sems, far_sem,
):
    copy = pltpu.make_async_copy(far_part_hbm, far_part_ref, far_sem)
    mix_kernel(
        True, head_ref, part_hbm, side_ref, rise_ref, start_ref, out_hbm,
        held_ref, ready_ref, part_ref, in_sems, out_sems, copy,
    )


def far_mix_kernel(part_ref, side_ref, rise_ref, start_ref, _, *rest):
    out_hbm, held_ref, ready_ref, out_sems = rest
    mix_kernel(
        False, None, None, side_ref, rise_ref, start_ref, out_hbm,
        held_ref, ready_ref, part_ref, None, out_sems, None,
    )


def mix_kernel(
    own, head_ref, part_hbm, side_ref, rise_ref, start_ref, out_hbm,
    held_ref, ready_ref, part_ref, in_sems, out_sems, next_copy,
):
    half = half_of(own)

    def part_copy(t):
        return pltpu.make_async_copy(
            part_hbm.at[t], part_ref.at[t], in_sems.at[t]
        )

    def out_copy(t):
        lanes = pl.ds(pl.multiple_of(half * (INNER // 2) + t * TILE, TILE), TILE)
        return pltpu.make_async_copy(ready_ref.at[t], out_hbm.at[:, lanes], out_sems.at[t])

    if own:
        for t in range(HEAD_TILES, HALF_TILES):
            part_copy(t).start()
        next_copy.start()
    unpack(start_ref, held_ref)
    for t in range(HALF_TILES):
        wide = spread(half * HALF_TILES + t)
        state = state_tile(held_ref, t).astype(BF16)
        tile_ref = part_ref.at[t]
        if own and t < HEAD_TILES:
            tile_ref = head_ref.at[t]
        elif own:
            part_copy(t).wait()
        for q in range(CHUNKS):
            span = slice(q * CHUNK, (q + 1) * CHUNK)
            carried = dot(side_ref[span, N_STATE:], state)
            ready_ref[t, span, :] = (
                tile_ref[span, :].astype(F32) + dot(rise_ref[span, :], wide) * carried
            ).astype(BF16)
        out_copy(t).start()
    for t in range(HALF_TILES):
        out_copy(t).wait()
    if own:
        next_copy.wait()


VMEM = pl.BlockSpec(memory_space=pltpu.VMEM)
HBM = pl.BlockSpec(memory_space=pltpu.HBM)


def params(limit):
    return pltpu.CompilerParams(vmem_limit_bytes=limit * MIB)


def in_hbm(value):
    return pltpu.with_memory_space_constraint(value, pltpu.HBM)


def body(xbc, conv_weight, conv_bias, dt, decay_log, skip):
    count = lax.axis_size(ALL)
    chips = count // 2
    swap = [(i, i ^ 1) for i in range(lax.axis_size("narrow"))]
    onward = [(i, i + 1) for i in range(0, lax.axis_size("narrow"), 2)]
    groups = [[2 * c + k for c in range(chips)] for k in range(2)]
    state_out = pltpu.VMEM((PAIRS, SENT, LANES), BF16)
    state_hbm = pltpu.HBM((PAIRS, SENT, LANES), BF16)
    half_out = pltpu.HBM((HALF_TILES, TOK, TILE), BF16)
    held = pltpu.VMEM((PAIRS * ROWS, LANES), F32)
    tiles_16 = pltpu.VMEM((HALF_TILES, TOK, TILE), BF16)
    tile_sems = pltpu.SemaphoreType.DMA((HALF_TILES,))
    inputs_out = jax.ShapeDtypeStruct((N_STATE, TOK), BF16)
    pair_out = jax.ShapeDtypeStruct((TOK, 2 * LANES), BF16)

    rim = lax.ppermute(xbc[TOK - 8 :], ALL, [(i, i + 1) for i in range(count - 1)])
    x_near, to_end, tail, factors, halves, level = pl.pallas_call(
        fetch_kernel,
        in_specs=[HBM, VMEM, VMEM, VMEM],
        out_specs=[VMEM] * 6,
        out_shape=[
            pltpu.VMEM((TOK, WIDTH), BF16),
            pair_out,
            pltpu.VMEM((8, LANES), F32),
            jax.ShapeDtypeStruct((TOK, 4 * LANES), BF16),
            jax.ShapeDtypeStruct((8 * CHUNKS + 8, 2 * LANES), BF16),
            jax.ShapeDtypeStruct((TOK, LANES), F32),
        ],
        scratch_shapes=[pltpu.SemaphoreType.DMA],
        compiler_params=params(8),
        name="fetch",
    )(in_hbm(xbc), in_hbm(dt), in_hbm(decay_log), skip[None, :])
    bias = conv_bias[None, :]
    state_scratch = [
        pltpu.VMEM((2 * GROUPS, 8 + TOK, LANES), F32),
        held,
        pltpu.VMEM((2, TOK, TILE), F32),
        pltpu.VMEM((2, TOK, TILE), BF16),
        tiles_16,
        pltpu.SemaphoreType.DMA((HALF_TILES + 1,)),
    ]
    values_far, other, side, inputs = pl.pallas_call(
        far_state_kernel,
        in_specs=[VMEM] * 6,
        out_specs=[HBM, VMEM, VMEM, VMEM],
        out_shape=[half_out, state_out, pair_out, inputs_out],
        scratch_shapes=state_scratch,
        compiler_params=params(16),
        name="far_states",
    )(x_near, rim, conv_weight, bias, to_end, tail)
    got = lax.ppermute(other, "narrow", swap)
    x_near, other = lax.optimization_barrier((x_near, other))
    values_own, mine, spare = pl.pallas_call(
        lambda *refs: state_kernel(True, *refs),
        in_specs=[VMEM] * 7,
        out_specs=[HBM, VMEM, HBM],
        out_shape=[half_out, state_out, state_hbm],
        scratch_shapes=state_scratch,
        compiler_params=params(16),
        cost_estimate=pl.CostEstimate(flops=2 * 10**9, bytes_accessed=10**7, transcendentals=0),
        name="own_states",
    )(x_near, rim, conv_weight, bias, to_end, tail, inputs)
    got, mine = lax.optimization_barrier((got, mine))
    joined, got = pl.pallas_call(
        join_kernel,
        in_specs=[VMEM] * 2,
        out_specs=[HBM, HBM],
        out_shape=[state_hbm, state_hbm],
        scratch_shapes=[
            pltpu.VMEM((PAIRS, SENT, LANES), BF16),
            pltpu.SemaphoreType.DMA((PAIRS // BATCH + 1,)),
        ],
        compiler_params=params(8),
        name="join_cores",
    )(mine, got)
    pieces = lax.all_to_all(joined, ALL, 0, 0, axis_index_groups=groups, tiled=True)
    joined, side = lax.optimization_barrier((joined, side))
    local_scratch = [
        held,
        pltpu.VMEM((CHUNKS, CHUNK, TILE), BF16),
        pltpu.VMEM((PAIRS, SENT, LANES), BF16),
        tiles_16,
        tiles_16,
        pltpu.VMEM((TOK, TILE), F32),
        pltpu.VMEM((TOK, TILE), F32),
        pltpu.SemaphoreType.DMA((HALF_TILES + 1,)),
        tile_sems,
    ]
    part_own, both, rise = pl.pallas_call(
        own_local_kernel,
        in_specs=[HBM] + [VMEM] * 5 + [HBM],
        out_specs=[HBM] + [VMEM] * 2,
        out_shape=[half_out, pair_out, pair_out],
        scratch_shapes=local_scratch,
        compiler_params=params(22),
        cost_estimate=pl.CostEstimate(flops=10**6, bytes_accessed=10**5, transcendentals=0),
        name="own_part",
    )(in_hbm(values_own), side, level, inputs, factors, halves, in_hbm(got))
    pieces, part_own = lax.optimization_barrier((pieces, part_own))
    prefixes = pl.pallas_call(
        lambda *refs: scan_kernel(chips, *refs),
        in_specs=[VMEM],
        out_specs=HBM,
        out_shape=pltpu.HBM((chips, ROWS, LANES), BF16),
        scratch_shapes=[
            pltpu.VMEM((chips, ROWS, LANES), BF16),
            pltpu.VMEM((chips * ROWS, LANES), F32),
            pltpu.SemaphoreType.DMA((chips // BATCH,)),
        ],
        compiler_params=params(12),
        name="scan_chips",
    )(pieces)
    own = lax.all_to_all(prefixes, ALL, 0, 0, axis_index_groups=groups, tiled=True)
    prefixes, values_far = lax.optimization_barrier((prefixes, values_far))
    prefixes, spare = lax.optimization_barrier((prefixes, spare))
    before = lax.ppermute(spare, "narrow", onward)
    part_far, head = pl.pallas_call(
        far_local_kernel,
        in_specs=[HBM] * 2 + [VMEM] * 4 + [HBM],
        out_specs=[HBM, VMEM],
        out_shape=[half_out, pltpu.VMEM((HEAD_TILES, TOK, TILE), BF16)],
        scratch_shapes=local_scratch + [pltpu.SemaphoreType.DMA],
        compiler_params=params(22),
        cost_estimate=pl.CostEstimate(flops=10**6, bytes_accessed=10**5, transcendentals=0),
        name="far_part",
    )(in_hbm(values_far), in_hbm(part_own), both, inputs, factors, halves, in_hbm(before))
    own, part_far = lax.optimization_barrier((own, part_far))
    across = lax.ppermute(own, "narrow", swap)

    out_type = jax.ShapeDtypeStruct((TOK, INNER), BF16)
    out, part_far = pl.pallas_call(
        own_mix_kernel,
        in_specs=[VMEM] + [HBM] * 2 + [VMEM] * 3,
        out_specs=[HBM, VMEM],
        out_shape=[out_type, pltpu.VMEM((HALF_TILES, TOK, TILE), BF16)],
        scratch_shapes=[
            held, tiles_16, tiles_16, tile_sems, tile_sems, pltpu.SemaphoreType.DMA
        ],
        compiler_params=params(16),
        cost_estimate=pl.CostEstimate(flops=10**9, bytes_accessed=10**7, transcendentals=0),
        name="own_mix",
    )(head, in_hbm(part_own), in_hbm(part_far), side, rise, own)
    across, out = lax.optimization_barrier((across, out))
    return pl.pallas_call(
        far_mix_kernel,
        in_specs=[VMEM] * 4 + [HBM],
        out_specs=HBM,
        out_shape=out_type,
        scratch_shapes=[held, tiles_16, tile_sems],
        input_output_aliases={4: 0},
        compiler_params=params(16),
        name="far_mix",
    )(part_far, side, rise, across, out)


def solution(mesh):
    placed = (P(ALL, None), P(), P(), P(None, ALL), P(None, ALL), P())
    return jax.shard_map(
        body, mesh=mesh, in_specs=placed, out_specs=P(ALL, None), check_vma=False
    )
```

```python
import jax
import jax.numpy as jnp
from jax import lax
from jax.experimental import pallas as pl
from jax.experimental.pallas import tpu as pltpu
from jax.sharding import PartitionSpec as P

HEADS = 80
HEAD_DIM = 64
N_STATE = 128
CONV = 4
INNER = 5120
WIDTH = INNER + 2 * N_STATE
TOK = 512
CHUNK = 128
CHUNKS = TOK // CHUNK
LANES = 128
TILE = 512
TILES = INNER // TILE
GROUPS = TILE // LANES
PIECE = 64
HALF_TILES = TILES // 2
HEAD_TILES = 2
BATCH = 16
HALF_GROUPS = INNER // LANES // 2
PAIRS = N_STATE // 2
ROWS = 2 * HALF_GROUPS
SENT = ROWS + 8
ALL = ("wide", "narrow")
F32 = jnp.float32
BF16 = jnp.bfloat16
MIB = 1024 * 1024


def dot(a, b):
    return jnp.dot(a, b, preferred_element_type=F32)


def dot_nt(a, b, precision=None):
    return lax.dot_general(
        a, b, (((1,), (1,)), ((), ())), preferred_element_type=F32, precision=precision
    )


def iota(shape, dim):
    return lax.broadcasted_iota(jnp.int32, shape, dim)


def split_pair(value):
    high = value.astype(BF16)
    low = (value - high.astype(F32)).astype(BF16)
    return jnp.concatenate([high, low], axis=1)


def pad_heads(value):
    return jnp.concatenate(
        [value, jnp.zeros((value.shape[0], LANES - HEADS), value.dtype)], axis=1
    )


def spread(tile):
    head = iota((2 * LANES, TILE), 0) % LANES
    lane = iota((2 * LANES, TILE), 1) // HEAD_DIM
    return (head == lane + tile * (TILE // HEAD_DIM)).astype(F32).astype(BF16)


def core_index():
    return lax.rem(lax.axis_index("narrow"), 2)


def running_decay(log_ref, dt_ref, chunk):
    rows, cols = iota((CHUNK, CHUNK), 0), iota((CHUNK, CHUNK), 1)
    lower = (rows >= cols).astype(F32)
    unit = (rows == cols).astype(F32)
    span = slice(chunk * CHUNK, (chunk + 1) * CHUNK)
    cumulative = dot_nt(lower, log_ref[:, span], lax.Precision.HIGHEST)
    steps = dot_nt(unit, dt_ref[:, span], lax.Precision.HIGHEST)
    return cumulative, steps


def thirds(row):
    high = row.astype(BF16).astype(F32)
    middle = (row - high).astype(BF16).astype(F32)
    low = row - high - middle
    return jnp.concatenate([high, middle, low, jnp.zeros((5, LANES), F32)], axis=0)


def half_lanes(half):
    return pl.ds(pl.multiple_of(half * (INNER // 2), LANES), INNER // 2)


def fetch_kernel(
    x_hbm, weight_hbm, bias_ref, dt_ref, log_ref, skip_ref,
    x_ref, x_side_ref, weight_ref, bias_row_ref,
    to_end_ref, tail_ref, factors_ref, halves_ref, level_ref, sems,
):
    copies = [
        pltpu.make_async_copy(weight_hbm, weight_ref, sems.at[0]),
        pltpu.make_async_copy(x_hbm.at[:, INNER:WIDTH], x_side_ref, sems.at[1]),
        pltpu.make_async_copy(x_hbm.at[:, half_lanes(half_of(False))], x_ref, sems.at[2]),
    ]
    for copy in copies:
        copy.start()
    for lane in range(0, WIDTH, LANES):
        bias_row_ref[:, lane : lane + LANES] = bias_ref[lane : lane + LANES][None, :]
    decays = [running_decay(log_ref, dt_ref, q) for q in range(CHUNKS)]
    totals = [cumulative[CHUNK - 1 :, :] for cumulative, _ in decays]
    after = jnp.zeros((1, HEADS), F32)
    for q in reversed(range(CHUNKS)):
        cumulative, steps = decays[q]
        to_end = jnp.exp(totals[q] - cumulative + after) * steps
        to_end_ref[q * CHUNK : (q + 1) * CHUNK, :] = split_pair(pad_heads(to_end))
        after = after + totals[q]
    tail_ref[...] = thirds(pad_heads(jnp.exp(after)))
    before = jnp.zeros((1, HEADS), F32)
    for q in range(CHUNKS):
        span = slice(q * CHUNK, (q + 1) * CHUNK)
        cumulative, steps = decays[q]
        middle = 0.5 * totals[q]
        factors_ref[span, 0 : 2 * LANES] = split_pair(
            pad_heads(jnp.exp(middle - cumulative) * steps)
        )
        factors_ref[span, 2 * LANES :] = split_pair(pad_heads(jnp.exp(cumulative - middle)))
        level_ref[span, :] = pad_heads(jnp.exp(cumulative + before))
        before = before + totals[q]
        halves_ref[8 * q : 8 * q + 8, :] = split_pair(
            jnp.broadcast_to(pad_heads(jnp.exp(middle)), (8, LANES))
        )
    halves_ref[8 * CHUNKS :, :] = split_pair(jnp.broadcast_to(pad_heads(skip_ref[...]), (8, LANES)))
    for copy in copies:
        copy.wait()


def conv_lanes(x_ref, rim_ref, weight_ref, bias_ref, span_ref, x_lane, lane, after):
    x_lanes = pl.ds(x_lane, LANES)
    lanes = pl.ds(lane, LANES)
    span_ref[0:8, :] = rim_ref[:, lanes].astype(F32)
    for row in range(0, TOK, PIECE):
        span_ref[8 + row : 8 + row + PIECE, :] = x_ref[row : row + PIECE, x_lanes].astype(F32)
    taps = [0.5 * weight_ref[k : k + 1, lanes] for k in range(CONV)]
    start = 0.5 * bias_ref[:, lanes]
    for row in range(0, TOK, PIECE):
        half = start
        for k in range(CONV):
            half = half + span_ref[5 + k + row : 5 + k + row + PIECE, :] * taps[k]
        after((half + half * jnp.tanh(half)).astype(BF16), row)


def half_of(own):
    return core_index() if own else 1 - core_index()


def side_values(x_ref, rim_ref, weight_ref, bias_ref, span_ref, side_ref, inputs_ref):
    for g in range(2):

        def keep(values, row, g=g):
            side_ref[row : row + PIECE, g * LANES : (g + 1) * LANES] = values

        conv_lanes(
            x_ref, rim_ref, weight_ref, bias_ref, span_ref.at[g], g * LANES,
            INNER + g * LANES, keep,
        )
    inputs_ref[...] = side_ref[:, 0:N_STATE].astype(F32).T.astype(BF16)


def state_kernel(
    own, x_ref, rim_ref, weight_ref, bias_ref, to_end_ref, tail_ref, inputs_ref,
    values_hbm, state_ref, *rest,
):
    span_ref, held_ref, scale_ref, loaded_ref, values_ref, sems = rest[-6:]
    spare_hbm = rest[0]
    half = half_of(own)

    def values_copy(t):
        return pltpu.make_async_copy(
            values_ref.at[t], values_hbm.at[t], sems.at[t]
        )

    def load(t, slot):
        scale_ref[slot] = dot(to_end_ref[...], spread(half * HALF_TILES + t))
        for g in range(GROUPS):
            x_lane = pl.multiple_of(t * TILE + g * LANES, LANES)
            lane = pl.multiple_of(half * (INNER // 2) + t * TILE + g * LANES, LANES)
            local = slice(g * LANES, (g + 1) * LANES)

            def keep(values, row, local=local):
                piece = slice(row, row + PIECE)
                values_ref[t, piece, local] = values
                loaded_ref[slot, piece, local] = (
                    values.astype(F32) * scale_ref[slot, piece, local]
                ).astype(BF16)

            conv_lanes(
                x_ref, rim_ref, weight_ref, bias_ref, span_ref.at[slot * GROUPS + g],
                x_lane, lane, keep,
            )
        values_copy(t).start()

    def finish(t, slot):
        state = dot(inputs_ref[...], loaded_ref[slot])
        for g in range(GROUPS):
            first = t * GROUPS + g
            part = state[:, g * LANES : (g + 1) * LANES]
            held_ref[pl.ds(first, PAIRS, stride=ROWS), :] = part[0:PAIRS]
            held_ref[pl.ds(first + HALF_GROUPS, PAIRS, stride=ROWS), :] = part[PAIRS:]

    load(0, 0)

    def step(pair, _):
        load(2 * pair + 1, 1)
        finish(2 * pair, 0)
        load(2 * pair + 2, 0)
        finish(2 * pair + 1, 1)
        return 0

    lax.fori_loop(0, HALF_TILES // 2, step, 0)
    finish(HALF_TILES - 1, 0)
    state_ref[:, ROWS:, :] = jnp.broadcast_to(tail_ref[...][None], (PAIRS, 8, LANES)).astype(BF16)

    def move(n, _):
        first = pl.multiple_of(n * ROWS, 8)
        state_ref[n, 0:ROWS, :] = held_ref[pl.ds(first, ROWS), :].astype(BF16)
        return 0

    lax.fori_loop(0, PAIRS, move, 0, unroll=8)
    if own:
        state_copy = pltpu.make_async_copy(state_ref, spare_hbm, sems.at[HALF_TILES])
        state_copy.start()
    for t in range(HALF_TILES):
        values_copy(t).wait()
    if own:
        state_copy.wait()


def far_state_kernel(
    x_ref, x_side_ref, x_hbm, rim_ref, weight_ref, bias_ref, to_end_ref, tail_ref,
    values_hbm, state_ref, side_ref, inputs_ref, x_own_ref, span_ref, *scratch,
):
    copy = pltpu.make_async_copy(x_hbm.at[:, half_lanes(half_of(True))], x_own_ref, scratch[-1])
    copy.start()
    side_values(x_side_ref, rim_ref, weight_ref, bias_ref, span_ref, side_ref, inputs_ref)
    state_kernel(
        False, x_ref, rim_ref, weight_ref, bias_ref, to_end_ref, tail_ref, inputs_ref,
        values_hbm, state_ref, span_ref, *scratch[:-1],
    )
    copy.wait()


def rows_of_heads(count, core):
    row = lax.rem(iota((count, ROWS, LANES), 1), HALF_GROUPS)
    head = iota((count, ROWS, LANES), 2)
    return (head // 2 == row + core * HALF_GROUPS).astype(F32)


def lanes_of_heads():
    head = iota((2 * LANES, LANES), 0)
    return (lax.rem(head, 2) == iota((2 * LANES, LANES), 1) // HEAD_DIM).astype(F32).astype(BF16)


def decay_rows(high, middle, count, core):
    mask = rows_of_heads(count, core)
    both = jnp.concatenate([mask * high, mask * middle], axis=2).astype(BF16)
    return dot(both.reshape(count * ROWS, 2 * LANES), lanes_of_heads())


def join_kernel(mine_ref, got_ref, out_hbm, got_hbm, out_ref, sems):
    core = core_index()
    copy = pltpu.make_async_copy(got_ref, got_hbm, sems.at[PAIRS // BATCH])
    copy.start()

    def out_copy(batch):
        some = pl.ds(batch * BATCH, BATCH)
        return pltpu.make_async_copy(out_ref.at[some], out_hbm.at[some], sems.at[batch])

    def join(first_ref, second_ref):
        first = first_ref[0, ROWS:, :].astype(F32)
        second = second_ref[0, ROWS:, :].astype(F32)
        decay = decay_rows(second[None, 0:1, :], second[None, 1:2, :], 1, core)
        whole = (first[0:1] + first[1:2] + first[2:3]) * (second[0:1] + second[1:2] + second[2:3])
        out_ref[:, ROWS:, :] = jnp.broadcast_to(thirds(whole)[None], (PAIRS, 8, LANES)).astype(BF16)

        def step(n, _):
            out_ref[n, 0:ROWS, :] = (
                decay * first_ref[n, 0:ROWS, :].astype(F32) + second_ref[n, 0:ROWS, :].astype(F32)
            ).astype(BF16)
            return 0

        def some(batch, _):
            lax.fori_loop(0, BATCH, lambda i, c: step(batch * BATCH + i, c), 0, unroll=4)
            out_copy(batch).start()
            return 0

        lax.fori_loop(0, PAIRS // BATCH, some, 0)

    pl.when(core == 0)(lambda: join(mine_ref, got_ref))
    pl.when(core == 1)(lambda: join(got_ref, mine_ref))
    for batch in range(PAIRS // BATCH):
        out_copy(batch).wait()
    copy.wait()


def scan_kernel(count, pieces_ref, out_hbm, out_ref, decay_ref, sems):
    tails = pieces_ref[:, ROWS:, :].astype(F32)
    decay_ref[...] = decay_rows(tails[:, 0:1, :], tails[:, 1:2, :], count, core_index())

    def out_copy(batch):
        some = pl.ds(batch * BATCH, BATCH)
        return pltpu.make_async_copy(out_ref.at[some], out_hbm.at[some], sems.at[batch])

    def step(i, running):
        out_ref[i] = running.astype(BF16)
        piece = pieces_ref[i, 0:ROWS, :].astype(F32)
        return decay_ref[pl.ds(pl.multiple_of(i * ROWS, 8), ROWS), :] * running + piece

    def some(batch, running):
        running = lax.fori_loop(
            0, BATCH, lambda i, held: step(batch * BATCH + i, held), running, unroll=4
        )
        out_copy(batch).start()
        return running

    lax.fori_loop(0, count // BATCH, some, jnp.zeros((ROWS, LANES), F32))
    for batch in range(count // BATCH):
        out_copy(batch).wait()


def unpack(state_ref, held_ref):
    def move(n, _):
        first = pl.multiple_of(n * ROWS, 8)
        held_ref[pl.ds(first, ROWS), :] = state_ref[n, 0:ROWS, :].astype(F32)
        return 0

    lax.fori_loop(0, PAIRS, move, 0, unroll=8)


def state_tile(held_ref, t):
    parts = []
    for g in range(GROUPS):
        first = t * GROUPS + g
        parts.append(
            jnp.concatenate(
                [
                    held_ref[pl.ds(first, PAIRS, stride=ROWS), :],
                    held_ref[pl.ds(first + HALF_GROUPS, PAIRS, stride=ROWS), :],
                ],
                axis=0,
            )
        )
    return jnp.concatenate(parts, axis=1)


def shared_scores(side_ref, both_ref):
    side = side_ref[...]
    rows, cols = iota((CHUNK, CHUNK), 0), iota((CHUNK, CHUNK), 1)
    for q in range(CHUNKS):
        span = slice(q * CHUNK, (q + 1) * CHUNK)
        readout = side[span, N_STATE:]
        scores = dot_nt(readout, side[span, 0:N_STATE])
        both_ref[span, 0:CHUNK] = jnp.where(rows >= cols, scores, 0.0).astype(BF16)
        both_ref[span, CHUNK:] = readout


def far_local_kernel(
    values_hbm, part_own_hbm, both_ref, inputs_ref, factors_ref, halves_ref, start_hbm,
    part_hbm, head_ref, *scratch,
):
    copy = pltpu.make_async_copy(part_own_hbm.at[0:HEAD_TILES], head_ref, scratch[-1])
    copy.start()
    local_kernel(
        False, None, values_hbm, both_ref, inputs_ref, factors_ref, halves_ref, start_hbm,
        part_hbm, *scratch[:-1],
    )
    copy.wait()


def own_local_kernel(
    values_hbm, side_ref, level_ref, inputs_ref, factors_ref, halves_ref, start_hbm,
    part_hbm, both_ref, rise_ref,
    *scratch,
):
    def prepare(start_ref):
        tail = start_ref[0, ROWS:, :].astype(F32)
        first_decay = jnp.where(core_index() == 0, 1.0, tail[0:1] + tail[1:2] + tail[2:3])
        rise_ref[...] = split_pair(level_ref[...] * first_decay)
        shared_scores(side_ref, both_ref)

    local_kernel(
        True, prepare, values_hbm, both_ref, inputs_ref, factors_ref, halves_ref, start_hbm,
        part_hbm, *scratch,
    )


def local_kernel(
    own, prepare, values_hbm, both_ref, inputs_ref, factors_ref, halves_ref, start_hbm,
    part_hbm,
    held_ref, scaled_ref, start_ref, values_ref, part_ref, scale_ref, rise_ref, in_sems, out_sems,
):
    half = half_of(own)
    start_copy = pltpu.make_async_copy(start_hbm, start_ref, in_sems.at[HALF_TILES])
    start_copy.start()

    def values_copy(t):
        return pltpu.make_async_copy(
            values_hbm.at[t], values_ref.at[t], in_sems.at[t]
        )

    def part_copy(t):
        return pltpu.make_async_copy(
            part_ref.at[t], part_hbm.at[t], out_sems.at[t]
        )

    for t in range(HALF_TILES):
        values_copy(t).start()
    start_copy.wait()
    if own:
        prepare(start_ref)

    @pl.when(core_index() == 0)
    def _():
        held_ref[...] = jnp.zeros_like(held_ref)

    pl.when(core_index() == 1)(lambda: unpack(start_ref, held_ref))
    for t in range(HALF_TILES):
        wide = spread(half * HALF_TILES + t)
        halves = dot(halves_ref[...], wide)
        skips = halves[8 * CHUNKS : 8 * CHUNKS + 1, :]
        state = state_tile(held_ref, t)
        values_copy(t).wait()
        scale_ref[...] = dot(factors_ref[:, 0 : 2 * LANES], wide)
        rise_ref[...] = dot(factors_ref[:, 2 * LANES :], wide)
        for q in range(CHUNKS):
            span = slice(q * CHUNK, (q + 1) * CHUNK)
            values = values_ref[t, span, :].astype(F32)
            scaled_ref[q] = (values * scale_ref[span, :]).astype(BF16)
            step = halves[8 * q : 8 * q + 1, :]
            begin = step * state
            mixed = dot(
                both_ref[span, :], jnp.concatenate([scaled_ref[q], begin.astype(BF16)], axis=0)
            )
            part_ref[t, span, :] = (mixed * rise_ref[span, :] + skips * values).astype(BF16)
            if q < CHUNKS - 1:
                state = step * (begin + dot(inputs_ref[:, span], scaled_ref[q]))
        part_copy(t).start()
    for t in range(HALF_TILES):
        part_copy(t).wait()


def own_mix_kernel(
    head_ref, part_hbm, far_part_hbm, side_ref, rise_ref, start_ref,
    out_hbm, far_part_ref, held_ref, ready_ref, part_ref, in_sems, out_sems, far_sem,
):
    copy = pltpu.make_async_copy(far_part_hbm, far_part_ref, far_sem)
    mix_kernel(
        True, head_ref, part_hbm, side_ref, rise_ref, start_ref, out_hbm,
        held_ref, ready_ref, part_ref, in_sems, out_sems, copy,
    )


def far_mix_kernel(part_ref, side_ref, rise_ref, start_ref, _, *rest):
    out_hbm, held_ref, ready_ref, out_sems = rest
    mix_kernel(
        False, None, None, side_ref, rise_ref, start_ref, out_hbm,
        held_ref, ready_ref, part_ref, None, out_sems, None,
    )


def mix_kernel(
    own, head_ref, part_hbm, side_ref, rise_ref, start_ref, out_hbm,
    held_ref, ready_ref, part_ref, in_sems, out_sems, next_copy,
):
    half = half_of(own)

    def part_copy(t):
        return pltpu.make_async_copy(
            part_hbm.at[t], part_ref.at[t], in_sems.at[t]
        )

    def out_copy(t):
        lanes = pl.ds(pl.multiple_of(half * (INNER // 2) + t * TILE, TILE), TILE)
        return pltpu.make_async_copy(ready_ref.at[t], out_hbm.at[:, lanes], out_sems.at[t])

    if own:
        for t in range(HEAD_TILES, HALF_TILES):
            part_copy(t).start()
        next_copy.start()
    unpack(start_ref, held_ref)
    for t in range(HALF_TILES):
        wide = spread(half * HALF_TILES + t)
        state = state_tile(held_ref, t).astype(BF16)
        tile_ref = part_ref.at[t]
        if own and t < HEAD_TILES:
            tile_ref = head_ref.at[t]
        elif own:
            part_copy(t).wait()
        for q in range(CHUNKS):
            span = slice(q * CHUNK, (q + 1) * CHUNK)
            carried = dot(side_ref[span, N_STATE:], state)
            ready_ref[t, span, :] = (
                tile_ref[span, :].astype(F32) + dot(rise_ref[span, :], wide) * carried
            ).astype(BF16)
        out_copy(t).start()
    for t in range(HALF_TILES):
        out_copy(t).wait()
    if own:
        next_copy.wait()


VMEM = pl.BlockSpec(memory_space=pltpu.VMEM)
HBM = pl.BlockSpec(memory_space=pltpu.HBM)


def params(limit):
    return pltpu.CompilerParams(vmem_limit_bytes=limit * MIB)


def in_hbm(value):
    return pltpu.with_memory_space_constraint(value, pltpu.HBM)


def body(xbc, conv_weight, conv_bias, dt, decay_log, skip):
    count = lax.axis_size(ALL)
    chips = count // 2
    swap = [(i, i ^ 1) for i in range(lax.axis_size("narrow"))]
    onward = [(i, i + 1) for i in range(0, lax.axis_size("narrow"), 2)]
    groups = [[2 * c + k for c in range(chips)] for k in range(2)]
    state_out = pltpu.VMEM((PAIRS, SENT, LANES), BF16)
    state_hbm = pltpu.HBM((PAIRS, SENT, LANES), BF16)
    half_out = pltpu.HBM((HALF_TILES, TOK, TILE), BF16)
    held = pltpu.VMEM((PAIRS * ROWS, LANES), F32)
    tiles_16 = pltpu.VMEM((HALF_TILES, TOK, TILE), BF16)
    tile_sems = pltpu.SemaphoreType.DMA((HALF_TILES,))
    inputs_out = jax.ShapeDtypeStruct((N_STATE, TOK), BF16)
    pair_out = jax.ShapeDtypeStruct((TOK, 2 * LANES), BF16)

    rim = lax.ppermute(xbc[TOK - 8 :], ALL, [(i, i + 1) for i in range(count - 1)])
    x_half = pltpu.VMEM((TOK, INNER // 2), BF16)
    x_far, x_side, weight, bias, to_end, tail, factors, halves, level = pl.pallas_call(
        fetch_kernel,
        in_specs=[HBM, HBM] + [VMEM] * 4,
        out_specs=[VMEM] * 9,
        out_shape=[
            x_half,
            pltpu.VMEM((TOK, 2 * N_STATE), BF16),
            pltpu.VMEM((CONV, WIDTH), F32),
            pltpu.VMEM((1, WIDTH), F32),
            pair_out,
            pltpu.VMEM((8, LANES), F32),
            jax.ShapeDtypeStruct((TOK, 4 * LANES), BF16),
            jax.ShapeDtypeStruct((8 * CHUNKS + 8, 2 * LANES), BF16),
            jax.ShapeDtypeStruct((TOK, LANES), F32),
        ],
        scratch_shapes=[pltpu.SemaphoreType.DMA((3,))],
        compiler_params=params(8),
        name="fetch",
    )(
        in_hbm(xbc), in_hbm(conv_weight), in_hbm(conv_bias), in_hbm(dt), in_hbm(decay_log),
        in_hbm(skip[None, :]),
    )
    state_scratch = [
        pltpu.VMEM((2 * GROUPS, 8 + TOK, LANES), F32),
        held,
        pltpu.VMEM((2, TOK, TILE), F32),
        pltpu.VMEM((2, TOK, TILE), BF16),
        tiles_16,
        pltpu.SemaphoreType.DMA((HALF_TILES + 1,)),
    ]
    values_far, other, side, inputs, x_own = pl.pallas_call(
        far_state_kernel,
        in_specs=[VMEM, VMEM, HBM] + [VMEM] * 5,
        out_specs=[HBM] + [VMEM] * 4,
        out_shape=[half_out, state_out, pair_out, inputs_out, x_half],
        scratch_shapes=state_scratch + [pltpu.SemaphoreType.DMA],
        compiler_params=params(16),
        name="far_states",
    )(x_far, x_side, in_hbm(xbc), rim, weight, bias, to_end, tail)
    got = lax.ppermute(other, "narrow", swap)
    x_own, other = lax.optimization_barrier((x_own, other))
    values_own, mine, spare = pl.pallas_call(
        lambda *refs: state_kernel(True, *refs),
        in_specs=[VMEM] * 7,
        out_specs=[HBM, VMEM, HBM],
        out_shape=[half_out, state_out, state_hbm],
        scratch_shapes=state_scratch,
        compiler_params=params(16),
        cost_estimate=pl.CostEstimate(flops=2 * 10**9, bytes_accessed=10**7, transcendentals=0),
        name="own_states",
    )(x_own, rim, weight, bias, to_end, tail, inputs)
    got, mine = lax.optimization_barrier((got, mine))
    joined, got = pl.pallas_call(
        join_kernel,
        in_specs=[VMEM] * 2,
        out_specs=[HBM, HBM],
        out_shape=[state_hbm, state_hbm],
        scratch_shapes=[
            pltpu.VMEM((PAIRS, SENT, LANES), BF16),
            pltpu.SemaphoreType.DMA((PAIRS // BATCH + 1,)),
        ],
        compiler_params=params(8),
        name="join_cores",
    )(mine, got)
    pieces = lax.all_to_all(joined, ALL, 0, 0, axis_index_groups=groups, tiled=True)
    joined, side = lax.optimization_barrier((joined, side))
    local_scratch = [
        held,
        pltpu.VMEM((CHUNKS, CHUNK, TILE), BF16),
        pltpu.VMEM((PAIRS, SENT, LANES), BF16),
        tiles_16,
        tiles_16,
        pltpu.VMEM((TOK, TILE), F32),
        pltpu.VMEM((TOK, TILE), F32),
        pltpu.SemaphoreType.DMA((HALF_TILES + 1,)),
        tile_sems,
    ]
    part_own, both, rise = pl.pallas_call(
        own_local_kernel,
        in_specs=[HBM] + [VMEM] * 5 + [HBM],
        out_specs=[HBM] + [VMEM] * 2,
        out_shape=[half_out, pair_out, pair_out],
        scratch_shapes=local_scratch,
        compiler_params=params(22),
        cost_estimate=pl.CostEstimate(flops=10**6, bytes_accessed=10**5, transcendentals=0),
        name="own_part",
    )(in_hbm(values_own), side, level, inputs, factors, halves, in_hbm(got))
    pieces, part_own = lax.optimization_barrier((pieces, part_own))
    prefixes = pl.pallas_call(
        lambda *refs: scan_kernel(chips, *refs),
        in_specs=[VMEM],
        out_specs=HBM,
        out_shape=pltpu.HBM((chips, ROWS, LANES), BF16),
        scratch_shapes=[
            pltpu.VMEM((chips, ROWS, LANES), BF16),
            pltpu.VMEM((chips * ROWS, LANES), F32),
            pltpu.SemaphoreType.DMA((chips // BATCH,)),
        ],
        compiler_params=params(12),
        name="scan_chips",
    )(pieces)
    own = lax.all_to_all(prefixes, ALL, 0, 0, axis_index_groups=groups, tiled=True)
    prefixes, values_far = lax.optimization_barrier((prefixes, values_far))
    prefixes, spare = lax.optimization_barrier((prefixes, spare))
    before = lax.ppermute(spare, "narrow", onward)
    part_far, head = pl.pallas_call(
        far_local_kernel,
        in_specs=[HBM] * 2 + [VMEM] * 4 + [HBM],
        out_specs=[HBM, VMEM],
        out_shape=[half_out, pltpu.VMEM((HEAD_TILES, TOK, TILE), BF16)],
        scratch_shapes=local_scratch + [pltpu.SemaphoreType.DMA],
        compiler_params=params(22),
        cost_estimate=pl.CostEstimate(flops=10**6, bytes_accessed=10**5, transcendentals=0),
        name="far_part",
    )(in_hbm(values_far), in_hbm(part_own), both, inputs, factors, halves, in_hbm(before))
    own, part_far = lax.optimization_barrier((own, part_far))
    across = lax.ppermute(own, "narrow", swap)

    out_type = jax.ShapeDtypeStruct((TOK, INNER), BF16)
    out, part_far = pl.pallas_call(
        own_mix_kernel,
        in_specs=[VMEM] + [HBM] * 2 + [VMEM] * 3,
        out_specs=[HBM, VMEM],
        out_shape=[out_type, pltpu.VMEM((HALF_TILES, TOK, TILE), BF16)],
        scratch_shapes=[
            held, tiles_16, tiles_16, tile_sems, tile_sems, pltpu.SemaphoreType.DMA
        ],
        compiler_params=params(16),
        cost_estimate=pl.CostEstimate(flops=10**9, bytes_accessed=10**7, transcendentals=0),
        name="own_mix",
    )(head, in_hbm(part_own), in_hbm(part_far), side, rise, own)
    across, out = lax.optimization_barrier((across, out))
    return pl.pallas_call(
        far_mix_kernel,
        in_specs=[VMEM] * 4 + [HBM],
        out_specs=HBM,
        out_shape=out_type,
        scratch_shapes=[held, tiles_16, tile_sems],
        input_output_aliases={4: 0},
        compiler_params=params(16),
        name="far_mix",
    )(part_far, side, rise, across, out)


def solution(mesh):
    placed = (P(ALL, None), P(), P(), P(None, ALL), P(None, ALL), P())
    return jax.shard_map(
        body, mesh=mesh, in_specs=placed, out_specs=P(ALL, None), check_vma=False
    )
```

```python
import jax
import jax.numpy as jnp
from jax import lax
from jax.experimental import pallas as pl
from jax.experimental.pallas import tpu as pltpu
from jax.sharding import PartitionSpec as P

HEADS = 80
HEAD_DIM = 64
HEAD_SHIFT = 6
N_STATE = 128
CONV = 4
INNER = 5120
WIDTH = INNER + 2 * N_STATE
TOK = 512
CHUNK = 128
CHUNKS = TOK // CHUNK
LANES = 128
TILE = 512
TILES = INNER // TILE
GROUPS = TILE // LANES
PIECE = 64
HALF_TILES = TILES // 2
HEAD_TILES = 2
BATCH = 16
HALF_GROUPS = INNER // LANES // 2
PAIRS = N_STATE // 2
ROWS = 2 * HALF_GROUPS
SENT = ROWS + 8
ALL = ("wide", "narrow")
F32 = jnp.float32
BF16 = jnp.bfloat16
MIB = 1024 * 1024


def dot(a, b):
    return jnp.dot(a, b, preferred_element_type=F32)


def dot_nt(a, b, precision=None):
    return lax.dot_general(
        a, b, (((1,), (1,)), ((), ())), preferred_element_type=F32, precision=precision
    )


def iota(shape, dim):
    return lax.broadcasted_iota(jnp.int32, shape, dim)


def split_pair(value):
    high = value.astype(BF16)
    low = (value - high.astype(F32)).astype(BF16)
    return jnp.concatenate([high, low], axis=1)


def pad_heads(value):
    return jnp.concatenate(
        [value, jnp.zeros((value.shape[0], LANES - HEADS), value.dtype)], axis=1
    )


def spread(tile):
    head = lax.bitwise_and(iota((2 * LANES, TILE), 0), LANES - 1)
    lane = lax.shift_right_logical(iota((2 * LANES, TILE), 1), HEAD_SHIFT)
    return (head == lane + tile * (TILE // HEAD_DIM)).astype(F32).astype(BF16)


def core_index():
    return lax.rem(lax.axis_index("narrow"), 2)


def running_decay(log_ref, dt_ref, chunk):
    rows, cols = iota((CHUNK, CHUNK), 0), iota((CHUNK, CHUNK), 1)
    lower = (rows >= cols).astype(F32)
    unit = (rows == cols).astype(F32)
    span = slice(chunk * CHUNK, (chunk + 1) * CHUNK)
    cumulative = dot_nt(lower, log_ref[:, span], lax.Precision.HIGHEST)
    steps = dot_nt(unit, dt_ref[:, span], lax.Precision.HIGHEST)
    return cumulative, steps


def thirds(row):
    high = row.astype(BF16).astype(F32)
    middle = (row - high).astype(BF16).astype(F32)
    low = row - high - middle
    return jnp.concatenate([high, middle, low, jnp.zeros((5, LANES), F32)], axis=0)


def half_lanes(half):
    return pl.ds(pl.multiple_of(half * (INNER // 2), LANES), INNER // 2)


def fetch_kernel(
    x_hbm, weight_hbm, bias_ref, dt_ref, log_ref, skip_ref,
    x_ref, x_side_ref, weight_ref, bias_row_ref,
    to_end_ref, tail_ref, factors_ref, halves_ref, level_ref, sems,
):
    copies = [
        pltpu.make_async_copy(weight_hbm, weight_ref, sems.at[0]),
        pltpu.make_async_copy(x_hbm.at[:, INNER:WIDTH], x_side_ref, sems.at[1]),
        pltpu.make_async_copy(x_hbm.at[:, half_lanes(half_of(False))], x_ref, sems.at[2]),
    ]
    for copy in copies:
        copy.start()
    for lane in range(0, WIDTH, LANES):
        bias_row_ref[:, lane : lane + LANES] = bias_ref[lane : lane + LANES][None, :]
    decays = [running_decay(log_ref, dt_ref, q) for q in range(CHUNKS)]
    totals = [cumulative[CHUNK - 1 :, :] for cumulative, _ in decays]
    after = jnp.zeros((1, HEADS), F32)
    for q in reversed(range(CHUNKS)):
        cumulative, steps = decays[q]
        to_end = jnp.exp(totals[q] - cumulative + after) * steps
        to_end_ref[q * CHUNK : (q + 1) * CHUNK, :] = split_pair(pad_heads(to_end))
        after = after + totals[q]
    tail_ref[...] = thirds(pad_heads(jnp.exp(after)))
    before = jnp.zeros((1, HEADS), F32)
    for q in range(CHUNKS):
        span = slice(q * CHUNK, (q + 1) * CHUNK)
        cumulative, steps = decays[q]
        middle = 0.5 * totals[q]
        factors_ref[span, 0 : 2 * LANES] = split_pair(
            pad_heads(jnp.exp(middle - cumulative) * steps)
        )
        factors_ref[span, 2 * LANES :] = split_pair(pad_heads(jnp.exp(cumulative - middle)))
        level_ref[span, :] = pad_heads(jnp.exp(cumulative + before))
        before = before + totals[q]
        halves_ref[8 * q : 8 * q + 8, :] = split_pair(
            jnp.broadcast_to(pad_heads(jnp.exp(middle)), (8, LANES))
        )
    halves_ref[8 * CHUNKS :, :] = split_pair(jnp.broadcast_to(pad_heads(skip_ref[...]), (8, LANES)))
    for copy in copies:
        copy.wait()


def conv_lanes(x_ref, rim_ref, weight_ref, bias_ref, span_ref, x_lane, lane, after):
    x_lanes = pl.ds(x_lane, LANES)
    lanes = pl.ds(lane, LANES)
    span_ref[0:8, :] = rim_ref[:, lanes].astype(F32)
    for row in range(0, TOK, PIECE):
        span_ref[8 + row : 8 + row + PIECE, :] = x_ref[row : row + PIECE, x_lanes].astype(F32)
    taps = [0.5 * weight_ref[k : k + 1, lanes] for k in range(CONV)]
    start = 0.5 * bias_ref[:, lanes]
    for row in range(0, TOK, PIECE):
        half = start
        for k in range(CONV):
            half = half + span_ref[5 + k + row : 5 + k + row + PIECE, :] * taps[k]
        after(half + half * jnp.tanh(half), row)


def half_of(own):
    return core_index() if own else 1 - core_index()


def side_values(x_ref, rim_ref, weight_ref, bias_ref, span_ref, side_ref, inputs_ref):
    for g in range(2):

        def keep(values, row, g=g):
            side_ref[row : row + PIECE, g * LANES : (g + 1) * LANES] = values.astype(BF16)

        conv_lanes(
            x_ref, rim_ref, weight_ref, bias_ref, span_ref.at[g], g * LANES,
            INNER + g * LANES, keep,
        )
    inputs_ref[...] = side_ref[:, 0:N_STATE].astype(F32).T.astype(BF16)


def state_kernel(
    own, x_ref, rim_ref, weight_ref, bias_ref, to_end_ref, tail_ref, inputs_ref,
    values_hbm, state_ref, *rest,
):
    span_ref, held_ref, scale_ref, loaded_ref, values_ref, sems = rest[-6:]
    spare_hbm = rest[0]
    half = half_of(own)

    def values_copy(t):
        return pltpu.make_async_copy(
            values_ref.at[t], values_hbm.at[t], sems.at[t]
        )

    def load(t, slot):
        scale_ref[slot] = dot(to_end_ref[...], spread(half * HALF_TILES + t))
        for g in range(GROUPS):
            x_lane = pl.multiple_of(t * TILE + g * LANES, LANES)
            lane = pl.multiple_of(half * (INNER // 2) + t * TILE + g * LANES, LANES)
            local = slice(g * LANES, (g + 1) * LANES)

            def keep(values, row, local=local):
                piece = slice(row, row + PIECE)
                values_ref[t, piece, local] = values.astype(BF16)
                loaded_ref[slot, piece, local] = (
                    values * scale_ref[slot, piece, local]
                ).astype(BF16)

            conv_lanes(
                x_ref, rim_ref, weight_ref, bias_ref, span_ref.at[slot * GROUPS + g],
                x_lane, lane, keep,
            )
        values_copy(t).start()

    def finish(t, slot):
        state = dot(inputs_ref[...], loaded_ref[slot])
        for g in range(GROUPS):
            first = t * GROUPS + g
            part = state[:, g * LANES : (g + 1) * LANES]
            held_ref[pl.ds(first, PAIRS, stride=ROWS), :] = part[0:PAIRS]
            held_ref[pl.ds(first + HALF_GROUPS, PAIRS, stride=ROWS), :] = part[PAIRS:]

    load(0, 0)

    def step(pair, _):
        load(2 * pair + 1, 1)
        finish(2 * pair, 0)
        load(2 * pair + 2, 0)
        finish(2 * pair + 1, 1)
        return 0

    lax.fori_loop(0, HALF_TILES // 2, step, 0)
    finish(HALF_TILES - 1, 0)
    state_ref[:, ROWS:, :] = jnp.broadcast_to(tail_ref[...][None], (PAIRS, 8, LANES)).astype(BF16)

    def move(n, _):
        first = pl.multiple_of(n * ROWS, 8)
        state_ref[n, 0:ROWS, :] = held_ref[pl.ds(first, ROWS), :].astype(BF16)
        return 0

    lax.fori_loop(0, PAIRS, move, 0, unroll=8)
    if own:
        state_copy = pltpu.make_async_copy(state_ref, spare_hbm, sems.at[HALF_TILES])
        state_copy.start()
    for t in range(HALF_TILES):
        values_copy(t).wait()
    if own:
        state_copy.wait()


def far_state_kernel(
    x_ref, x_side_ref, x_hbm, rim_ref, weight_ref, bias_ref, to_end_ref, tail_ref,
    values_hbm, state_ref, side_ref, inputs_ref, x_own_ref, span_ref, *scratch,
):
    copy = pltpu.make_async_copy(x_hbm.at[:, half_lanes(half_of(True))], x_own_ref, scratch[-1])
    copy.start()
    side_values(x_side_ref, rim_ref, weight_ref, bias_ref, span_ref, side_ref, inputs_ref)
    state_kernel(
        False, x_ref, rim_ref, weight_ref, bias_ref, to_end_ref, tail_ref, inputs_ref,
        values_hbm, state_ref, span_ref, *scratch[:-1],
    )
    copy.wait()


def rows_of_heads(core):
    row = iota((ROWS, LANES), 0)
    row = jnp.where(row >= HALF_GROUPS, row - HALF_GROUPS, row)
    pair = lax.shift_right_logical(iota((ROWS, LANES), 1), 1)
    return (pair == row + core * HALF_GROUPS).astype(F32)[None]


def lanes_of_heads():
    head = iota((2 * LANES, LANES), 0)
    return (lax.rem(head, 2) == iota((2 * LANES, LANES), 1) // HEAD_DIM).astype(F32).astype(BF16)


def decay_rows(high, middle, count, core):
    mask = rows_of_heads(core)
    both = jnp.concatenate([mask * high, mask * middle], axis=2).astype(BF16)
    return dot(both.reshape(count * ROWS, 2 * LANES), lanes_of_heads())


def join_kernel(mine_ref, got_ref, out_hbm, got_hbm, out_ref, sems):
    core = core_index()
    copy = pltpu.make_async_copy(got_ref, got_hbm, sems.at[PAIRS // BATCH])
    copy.start()

    def out_copy(batch):
        some = pl.ds(batch * BATCH, BATCH)
        return pltpu.make_async_copy(out_ref.at[some], out_hbm.at[some], sems.at[batch])

    def join(first_ref, second_ref):
        first = first_ref[0, ROWS:, :].astype(F32)
        second = second_ref[0, ROWS:, :].astype(F32)
        decay = decay_rows(second[None, 0:1, :], second[None, 1:2, :], 1, core)
        whole = (first[0:1] + first[1:2] + first[2:3]) * (second[0:1] + second[1:2] + second[2:3])
        out_ref[:, ROWS:, :] = jnp.broadcast_to(thirds(whole)[None], (PAIRS, 8, LANES)).astype(BF16)

        def step(n, _):
            out_ref[n, 0:ROWS, :] = (
                decay * first_ref[n, 0:ROWS, :].astype(F32) + second_ref[n, 0:ROWS, :].astype(F32)
            ).astype(BF16)
            return 0

        def some(batch, _):
            lax.fori_loop(0, BATCH, lambda i, c: step(batch * BATCH + i, c), 0, unroll=4)
            out_copy(batch).start()
            return 0

        lax.fori_loop(0, PAIRS // BATCH, some, 0)

    pl.when(core == 0)(lambda: join(mine_ref, got_ref))
    pl.when(core == 1)(lambda: join(got_ref, mine_ref))
    for batch in range(PAIRS // BATCH):
        out_copy(batch).wait()
    copy.wait()


def scan_kernel(count, pieces_ref, out_hbm, out_ref, decay_ref, sems):
    tails = pieces_ref[:, ROWS:, :].astype(F32)
    decay_ref[...] = decay_rows(tails[:, 0:1, :], tails[:, 1:2, :], count, core_index())

    def out_copy(batch):
        some = pl.ds(batch * BATCH, BATCH)
        return pltpu.make_async_copy(out_ref.at[some], out_hbm.at[some], sems.at[batch])

    def step(i, running):
        out_ref[i] = running.astype(BF16)
        piece = pieces_ref[i, 0:ROWS, :].astype(F32)
        return decay_ref[pl.ds(pl.multiple_of(i * ROWS, 8), ROWS), :] * running + piece

    def some(batch, running):
        running = lax.fori_loop(
            0, BATCH, lambda i, held: step(batch * BATCH + i, held), running, unroll=4
        )
        out_copy(batch).start()
        return running

    lax.fori_loop(0, count // BATCH, some, jnp.zeros((ROWS, LANES), F32))
    for batch in range(count // BATCH):
        out_copy(batch).wait()


def unpack(state_ref, held_ref):
    def move(n, _):
        first = pl.multiple_of(n * ROWS, 8)
        held_ref[pl.ds(first, ROWS), :] = state_ref[n, 0:ROWS, :].astype(F32)
        return 0

    lax.fori_loop(0, PAIRS, move, 0, unroll=8)


def state_tile(held_ref, t):
    parts = []
    for g in range(GROUPS):
        first = t * GROUPS + g
        parts.append(
            jnp.concatenate(
                [
                    held_ref[pl.ds(first, PAIRS, stride=ROWS), :],
                    held_ref[pl.ds(first + HALF_GROUPS, PAIRS, stride=ROWS), :],
                ],
                axis=0,
            )
        )
    return jnp.concatenate(parts, axis=1)


def shared_scores(side_ref, both_ref):
    side = side_ref[...]
    rows, cols = iota((CHUNK, CHUNK), 0), iota((CHUNK, CHUNK), 1)
    for q in range(CHUNKS):
        span = slice(q * CHUNK, (q + 1) * CHUNK)
        readout = side[span, N_STATE:]
        scores = dot_nt(readout, side[span, 0:N_STATE])
        both_ref[span, 0:CHUNK] = jnp.where(rows >= cols, scores, 0.0).astype(BF16)
        both_ref[span, CHUNK:] = readout


def far_local_kernel(
    values_hbm, part_own_hbm, both_ref, inputs_ref, factors_ref, halves_ref, start_hbm,
    part_hbm, head_ref, *scratch,
):
    copy = pltpu.make_async_copy(part_own_hbm.at[0:HEAD_TILES], head_ref, scratch[-1])
    copy.start()
    local_kernel(
        False, None, values_hbm, both_ref, inputs_ref, factors_ref, halves_ref, start_hbm,
        part_hbm, *scratch[:-1],
    )
    copy.wait()


def own_local_kernel(
    values_hbm, side_ref, level_ref, inputs_ref, factors_ref, halves_ref, start_hbm,
    part_hbm, both_ref, rise_ref,
    *scratch,
):
    def prepare(start_ref):
        tail = start_ref[0, ROWS:, :].astype(F32)
        first_decay = jnp.where(core_index() == 0, 1.0, tail[0:1] + tail[1:2] + tail[2:3])
        rise_ref[...] = split_pair(level_ref[...] * first_decay)
        shared_scores(side_ref, both_ref)

    local_kernel(
        True, prepare, values_hbm, both_ref, inputs_ref, factors_ref, halves_ref, start_hbm,
        part_hbm, *scratch,
    )


def local_kernel(
    own, prepare, values_hbm, both_ref, inputs_ref, factors_ref, halves_ref, start_hbm,
    part_hbm,
    held_ref, scaled_ref, start_ref, values_ref, part_ref, scale_ref, rise_ref, in_sems, out_sems,
):
    half = half_of(own)
    start_copy = pltpu.make_async_copy(start_hbm, start_ref, in_sems.at[HALF_TILES])
    start_copy.start()

    def values_copy(t):
        return pltpu.make_async_copy(
            values_hbm.at[t], values_ref.at[t], in_sems.at[t]
        )

    def part_copy(t):
        return pltpu.make_async_copy(
            part_ref.at[t], part_hbm.at[t], out_sems.at[t]
        )

    for t in range(HALF_TILES):
        values_copy(t).start()
    start_copy.wait()
    if own:
        prepare(start_ref)

    @pl.when(core_index() == 0)
    def _():
        held_ref[...] = jnp.zeros_like(held_ref)

    pl.when(core_index() == 1)(lambda: unpack(start_ref, held_ref))
    for t in range(HALF_TILES):
        wide = spread(half * HALF_TILES + t)
        halves = dot(halves_ref[...], wide)
        skips = halves[8 * CHUNKS : 8 * CHUNKS + 1, :]
        state = state_tile(held_ref, t)
        values_copy(t).wait()
        scale_ref[...] = dot(factors_ref[:, 0 : 2 * LANES], wide)
        rise_ref[...] = dot(factors_ref[:, 2 * LANES :], wide)
        for q in range(CHUNKS):
            span = slice(q * CHUNK, (q + 1) * CHUNK)
            values = values_ref[t, span, :].astype(F32)
            scaled_ref[q] = (values * scale_ref[span, :]).astype(BF16)
            step = halves[8 * q : 8 * q + 1, :]
            begin = step * state
            mixed = dot(
                both_ref[span, :], jnp.concatenate([scaled_ref[q], begin.astype(BF16)], axis=0)
            )
            part_ref[t, span, :] = (mixed * rise_ref[span, :] + skips * values).astype(BF16)
            if q < CHUNKS - 1:
                state = step * (begin + dot(inputs_ref[:, span], scaled_ref[q]))
        part_copy(t).start()
    for t in range(HALF_TILES):
        part_copy(t).wait()


def own_mix_kernel(
    head_ref, part_hbm, far_part_hbm, side_ref, rise_ref, start_ref,
    out_hbm, far_part_ref, held_ref, ready_ref, part_ref, in_sems, out_sems, far_sem,
):
    copy = pltpu.make_async_copy(far_part_hbm, far_part_ref, far_sem)
    mix_kernel(
        True, head_ref, part_hbm, side_ref, rise_ref, start_ref, out_hbm,
        held_ref, ready_ref, part_ref, in_sems, out_sems, copy,
    )


def far_mix_kernel(part_ref, side_ref, rise_ref, start_ref, _, *rest):
    out_hbm, held_ref, ready_ref, out_sems = rest
    mix_kernel(
        False, None, None, side_ref, rise_ref, start_ref, out_hbm,
        held_ref, ready_ref, part_ref, None, out_sems, None,
    )


def mix_kernel(
    own, head_ref, part_hbm, side_ref, rise_ref, start_ref, out_hbm,
    held_ref, ready_ref, part_ref, in_sems, out_sems, next_copy,
):
    half = half_of(own)

    def part_copy(t):
        return pltpu.make_async_copy(
            part_hbm.at[t], part_ref.at[t], in_sems.at[t]
        )

    def out_copy(t):
        lanes = pl.ds(pl.multiple_of(half * (INNER // 2) + t * TILE, TILE), TILE)
        return pltpu.make_async_copy(ready_ref.at[t], out_hbm.at[:, lanes], out_sems.at[t])

    if own:
        for t in range(HEAD_TILES, HALF_TILES):
            part_copy(t).start()
        next_copy.start()
    unpack(start_ref, held_ref)
    for t in range(HALF_TILES):
        wide = spread(half * HALF_TILES + t)
        state = state_tile(held_ref, t).astype(BF16)
        tile_ref = part_ref.at[t]
        if own and t < HEAD_TILES:
            tile_ref = head_ref.at[t]
        elif own:
            part_copy(t).wait()
        for q in range(CHUNKS):
            span = slice(q * CHUNK, (q + 1) * CHUNK)
            carried = dot(side_ref[span, N_STATE:], state)
            ready_ref[t, span, :] = (
                tile_ref[span, :].astype(F32) + dot(rise_ref[span, :], wide) * carried
            ).astype(BF16)
        out_copy(t).start()
    for t in range(HALF_TILES):
        out_copy(t).wait()
    if own:
        next_copy.wait()


VMEM = pl.BlockSpec(memory_space=pltpu.VMEM)
HBM = pl.BlockSpec(memory_space=pltpu.HBM)


def params(limit):
    return pltpu.CompilerParams(vmem_limit_bytes=limit * MIB)


def in_hbm(value):
    return pltpu.with_memory_space_constraint(value, pltpu.HBM)


def body(xbc, conv_weight, conv_bias, dt, decay_log, skip):
    count = lax.axis_size(ALL)
    chips = count // 2
    swap = [(i, i ^ 1) for i in range(lax.axis_size("narrow"))]
    onward = [(i, i + 1) for i in range(0, lax.axis_size("narrow"), 2)]
    groups = [[2 * c + k for c in range(chips)] for k in range(2)]
    state_out = pltpu.VMEM((PAIRS, SENT, LANES), BF16)
    state_hbm = pltpu.HBM((PAIRS, SENT, LANES), BF16)
    half_out = pltpu.HBM((HALF_TILES, TOK, TILE), BF16)
    held = pltpu.VMEM((PAIRS * ROWS, LANES), F32)
    tiles_16 = pltpu.VMEM((HALF_TILES, TOK, TILE), BF16)
    tile_sems = pltpu.SemaphoreType.DMA((HALF_TILES,))
    inputs_out = jax.ShapeDtypeStruct((N_STATE, TOK), BF16)
    pair_out = jax.ShapeDtypeStruct((TOK, 2 * LANES), BF16)

    rim = lax.ppermute(xbc[TOK - 8 :], ALL, [(i, i + 1) for i in range(count - 1)])
    x_half = pltpu.VMEM((TOK, INNER // 2), BF16)
    x_far, x_side, weight, bias, to_end, tail, factors, halves, level = pl.pallas_call(
        fetch_kernel,
        in_specs=[HBM, HBM] + [VMEM] * 4,
        out_specs=[VMEM] * 9,
        out_shape=[
            x_half,
            pltpu.VMEM((TOK, 2 * N_STATE), BF16),
            pltpu.VMEM((CONV, WIDTH), F32),
            pltpu.VMEM((1, WIDTH), F32),
            pair_out,
            pltpu.VMEM((8, LANES), F32),
            jax.ShapeDtypeStruct((TOK, 4 * LANES), BF16),
            jax.ShapeDtypeStruct((8 * CHUNKS + 8, 2 * LANES), BF16),
            jax.ShapeDtypeStruct((TOK, LANES), F32),
        ],
        scratch_shapes=[pltpu.SemaphoreType.DMA((3,))],
        compiler_params=params(8),
        name="fetch",
    )(
        in_hbm(xbc), in_hbm(conv_weight), in_hbm(conv_bias), in_hbm(dt), in_hbm(decay_log),
        in_hbm(skip[None, :]),
    )
    state_scratch = [
        pltpu.VMEM((2 * GROUPS, 8 + TOK, LANES), F32),
        held,
        pltpu.VMEM((2, TOK, TILE), F32),
        pltpu.VMEM((2, TOK, TILE), BF16),
        tiles_16,
        pltpu.SemaphoreType.DMA((HALF_TILES + 1,)),
    ]
    values_far, other, side, inputs, x_own = pl.pallas_call(
        far_state_kernel,
        in_specs=[VMEM, VMEM, HBM] + [VMEM] * 5,
        out_specs=[HBM] + [VMEM] * 4,
        out_shape=[half_out, state_out, pair_out, inputs_out, x_half],
        scratch_shapes=state_scratch + [pltpu.SemaphoreType.DMA],
        compiler_params=params(16),
        name="far_states",
    )(x_far, x_side, in_hbm(xbc), rim, weight, bias, to_end, tail)
    got = lax.ppermute(other, "narrow", swap)
    x_own, other = lax.optimization_barrier((x_own, other))
    values_own, mine, spare = pl.pallas_call(
        lambda *refs: state_kernel(True, *refs),
        in_specs=[VMEM] * 7,
        out_specs=[HBM, VMEM, HBM],
        out_shape=[half_out, state_out, state_hbm],
        scratch_shapes=state_scratch,
        compiler_params=params(16),
        cost_estimate=pl.CostEstimate(flops=2 * 10**9, bytes_accessed=10**7, transcendentals=0),
        name="own_states",
    )(x_own, rim, weight, bias, to_end, tail, inputs)
    got, mine = lax.optimization_barrier((got, mine))
    joined, got = pl.pallas_call(
        join_kernel,
        in_specs=[VMEM] * 2,
        out_specs=[HBM, HBM],
        out_shape=[state_hbm, state_hbm],
        scratch_shapes=[
            pltpu.VMEM((PAIRS, SENT, LANES), BF16),
            pltpu.SemaphoreType.DMA((PAIRS // BATCH + 1,)),
        ],
        compiler_params=params(8),
        name="join_cores",
    )(mine, got)
    pieces = lax.all_to_all(joined, ALL, 0, 0, axis_index_groups=groups, tiled=True)
    joined, side = lax.optimization_barrier((joined, side))
    local_scratch = [
        held,
        pltpu.VMEM((CHUNKS, CHUNK, TILE), BF16),
        pltpu.VMEM((PAIRS, SENT, LANES), BF16),
        tiles_16,
        tiles_16,
        pltpu.VMEM((TOK, TILE), F32),
        pltpu.VMEM((TOK, TILE), F32),
        pltpu.SemaphoreType.DMA((HALF_TILES + 1,)),
        tile_sems,
    ]
    part_own, both, rise = pl.pallas_call(
        own_local_kernel,
        in_specs=[HBM] + [VMEM] * 5 + [HBM],
        out_specs=[HBM] + [VMEM] * 2,
        out_shape=[half_out, pair_out, pair_out],
        scratch_shapes=local_scratch,
        compiler_params=params(22),
        cost_estimate=pl.CostEstimate(flops=10**6, bytes_accessed=10**5, transcendentals=0),
        name="own_part",
    )(in_hbm(values_own), side, level, inputs, factors, halves, in_hbm(got))
    pieces, part_own = lax.optimization_barrier((pieces, part_own))
    prefixes = pl.pallas_call(
        lambda *refs: scan_kernel(chips, *refs),
        in_specs=[VMEM],
        out_specs=HBM,
        out_shape=pltpu.HBM((chips, ROWS, LANES), BF16),
        scratch_shapes=[
            pltpu.VMEM((chips, ROWS, LANES), BF16),
            pltpu.VMEM((chips * ROWS, LANES), F32),
            pltpu.SemaphoreType.DMA((chips // BATCH,)),
        ],
        compiler_params=params(12),
        name="scan_chips",
    )(pieces)
    own = lax.all_to_all(prefixes, ALL, 0, 0, axis_index_groups=groups, tiled=True)
    prefixes, values_far = lax.optimization_barrier((prefixes, values_far))
    prefixes, spare = lax.optimization_barrier((prefixes, spare))
    before = lax.ppermute(spare, "narrow", onward)
    part_far, head = pl.pallas_call(
        far_local_kernel,
        in_specs=[HBM] * 2 + [VMEM] * 4 + [HBM],
        out_specs=[HBM, VMEM],
        out_shape=[half_out, pltpu.VMEM((HEAD_TILES, TOK, TILE), BF16)],
        scratch_shapes=local_scratch + [pltpu.SemaphoreType.DMA],
        compiler_params=params(22),
        cost_estimate=pl.CostEstimate(flops=10**6, bytes_accessed=10**5, transcendentals=0),
        name="far_part",
    )(in_hbm(values_far), in_hbm(part_own), both, inputs, factors, halves, in_hbm(before))
    own, part_far = lax.optimization_barrier((own, part_far))
    across = lax.ppermute(own, "narrow", swap)

    out_type = jax.ShapeDtypeStruct((TOK, INNER), BF16)
    out, part_far = pl.pallas_call(
        own_mix_kernel,
        in_specs=[VMEM] + [HBM] * 2 + [VMEM] * 3,
        out_specs=[HBM, VMEM],
        out_shape=[out_type, pltpu.VMEM((HALF_TILES, TOK, TILE), BF16)],
        scratch_shapes=[
            held, tiles_16, tiles_16, tile_sems, tile_sems, pltpu.SemaphoreType.DMA
        ],
        compiler_params=params(16),
        cost_estimate=pl.CostEstimate(flops=10**9, bytes_accessed=10**7, transcendentals=0),
        name="own_mix",
    )(head, in_hbm(part_own), in_hbm(part_far), side, rise, own)
    across, out = lax.optimization_barrier((across, out))
    return pl.pallas_call(
        far_mix_kernel,
        in_specs=[VMEM] * 4 + [HBM],
        out_specs=HBM,
        out_shape=out_type,
        scratch_shapes=[held, tiles_16, tile_sems],
        input_output_aliases={4: 0},
        compiler_params=params(16),
        name="far_mix",
    )(part_far, side, rise, across, out)


def solution(mesh):
    placed = (P(ALL, None), P(), P(), P(None, ALL), P(None, ALL), P())
    return jax.shard_map(
        body, mesh=mesh, in_specs=placed, out_specs=P(ALL, None), check_vma=False
    )
```
